256 devices in a mesh: section: 16 (over x, z_lo, core), tensor: 16 (over z_hi, y).
Axes of the slice: x: 4, y: 4, z: 8 (z_hi: 4, z_lo: 2; z = z_hi * 2 + z_lo), core: 2. Of those that a mesh axis runs over, the one named last changes fastest.
Arguments:
- hidden: bfloat16 [8192, 14336], P('section', 'tensor'), may hold values from -6 to 6
- down_weight: bfloat16 [16, 14336, 4096], P('section', 'tensor'), may hold values from -0.046875 to 0.046875
- down_shrink: bfloat16 [16, 14336, 256], P('section', 'tensor'), may hold values from -0.046875 to 0.046875
- down_up_factors: bfloat16 [16, 256, 4096], P('section', None, 'tensor'), may hold values from -0.5 to 0.5
- residual: bfloat16 [8192, 4096], P(('section', 'tensor')), may hold values from -6 to 6
- tenant_ids: int32 [8192], P('section'), may hold values from 0 to 3
- adapter_rank: int32 [4], replicated, may hold values from 16 to 128, as said below
- adapter_offset: int32 [4], replicated, may hold values from 0 to 224, as said below
- norm_gain: bfloat16 [16, 4096], P('section'), may hold values from 0.099609375 to 1.8984375
- qkv_weight: bfloat16 [16, 4096, 5120], P('section', None, 'tensor'), may hold values from -0.09375 to 0.09375
- qkv_shrink: bfloat16 [16, 4096, 256], P('section', None, 'tensor'), may hold values from -0.09375 to 0.09375
- qkv_expand: bfloat16 [16, 256, 5120], P('section', None, 'tensor'), may hold values from -0.5 to 0.5
Outputs:
- stream: bfloat16 [8192, 4096], P(('section', 'tensor'))
- qkv: bfloat16 [8192, 5120], P('section', 'tensor')
The draws below stay inside these ranges and needn't reach their ends.
Inputs may be any that keep to these rules, and one draw needn't show every extreme that they name: `adapter_rank`: every rank is a multiple of 16; one tenant has rank 256 // 2, the last tenant has rank 256 // 16; the ranks sum to exactly 240. `adapter_offset`: the exclusive prefix sums of adapter_rank in tenant order.
All inputs are finite; a program needn't handle non-finite values.
Results may differ from the reference program's by a relative error of at most 0.02.
Values may be sent and summed in bfloat16 or wider, within the bound.
No kernel may reach another device: no remote copies, remote signals or barrier semaphores. Data moves between devices by JAX's collectives and lax.ppermute only.
A program may use at most 64 MiB of HBM per device.

```python
import math
import jax
import jax.numpy as jnp
import numpy as np
from jax import lax

D = 4096
FF = 14336
QKV = 5120
RANKS = 256
TENANTS = 4
ROWS = 512
SECTIONS = 16
TOTAL_ROWS = 8192
N_TENSOR = 16


def rank_table(key):
    unit = RANKS // 16
    order = jax.random.permutation(jax.random.fold_in(key, 11), 3)
    middle = jax.random.randint(jax.random.fold_in(key, 12), (), 1, 4) * unit
    slots = jnp.arange(TENANTS, dtype=jnp.int32)
    tenant_ranks = jnp.where(slots == TENANTS - 1, unit, jnp.where(slots == order[0], 8 * unit, jnp.where(slots == order[1], middle, 6 * unit - middle)))
    return tenant_ranks.astype(jnp.int32)


def draw_adapter_rank(key, part):
    tenant_ranks = rank_table(key)
    return tenant_ranks


def draw_adapter_offset(key, part):
    tenant_ranks = rank_table(key)
    return (jnp.cumsum(tenant_ranks) - tenant_ranks).astype(jnp.int32)


def set_ends(values, rng, least, top_value):
    spot = [jax.random.randint(jax.random.fold_in(rng, axis), (), 0, length) for axis, length in enumerate(values.shape)]
    longest = values.shape.index(max(values.shape))
    beside = spot[:longest] + [(spot[longest] + 1) % values.shape[longest]] + spot[longest + 1:]
    return values.at[tuple(spot)].set(least).at[tuple(beside)].set(top_value)


def level_of(stream_key, shape, split, least, top_value):
    loudness = 1.0
    for dim, blocks in split:
        heights = jax.random.uniform(jax.random.fold_in(jax.random.fold_in(stream_key, 6), dim), (blocks,), jnp.float32, least / len(split), top_value / len(split))
        loudness = loudness * jnp.repeat(jnp.exp(heights), shape[dim] // blocks).reshape((-1,) + (1,) * (len(shape) - 1 - dim))
    return loudness


def cumulative_ranks(number_of, lean):
    weights = [(1 << 20) // math.isqrt(grade ** lean) + 1 for grade in range(1, number_of + 1)]
    deviation = 1 + sum(weights) // (1 << 30)
    return np.cumsum(np.array([max(1, weight // deviation) for weight in weights]))


def ranked(rng, dims, amount, skew):
    grid = cumulative_ranks(amount, skew)
    lot = jax.random.randint(jax.random.fold_in(rng, 1), dims, 0, int(grid[amount - 1]))
    standing = jnp.searchsorted(jnp.asarray(grid, jnp.int32), lot, side="right")
    return jax.random.permutation(jax.random.fold_in(rng, 2), amount)[standing].astype(jnp.int32)


def bell_draw(rng, shape, width, most, cuts=(), kind=jnp.bfloat16):
    loudness = level_of(rng, shape, cuts, -0.22, 0.18) if cuts else 1.0
    values = jax.random.normal(rng, shape, jnp.float32) * width * loudness
    return jnp.minimum(jnp.maximum(values, -most), most).astype(kind)


def setup_inputs(seed: int = 0) -> dict:
    streams_of = jax.random.split(jax.random.key(seed), 13)
    return {
        "hidden": bell_draw(streams_of[0], (TOTAL_ROWS, FF), 1.0, 6.0, ((0, 16), (1, 16))),
        "down_weight": bell_draw(streams_of[1], (SECTIONS, FF, D), FF ** -0.5, 0.046875, ((0, 16), (1, 16))),
        "down_shrink": bell_draw(streams_of[2], (SECTIONS, FF, RANKS), FF ** -0.5, 0.046875, ((0, 16), (1, 16))),
        "down_up_factors": bell_draw(streams_of[3], (SECTIONS, RANKS, D), 128 ** -0.5, 0.5, ((0, 16), (2, 16))),
        "residual": bell_draw(streams_of[4], (TOTAL_ROWS, D), 1.0, 6.0, ((0, 256),)),
        "tenant_ids": set_ends(ranked(streams_of[5], (TOTAL_ROWS,), TENANTS, 2), jax.random.fold_in(streams_of[5], 3), 0, TENANTS - 1).astype(jnp.int32),
        "adapter_rank": draw_adapter_rank(jax.random.fold_in(streams_of[12], 71), 0),
        "adapter_offset": draw_adapter_offset(jax.random.fold_in(streams_of[12], 71), 0),
        "norm_gain": jnp.clip(1.0 + 0.18 * jax.random.normal(streams_of[8], (SECTIONS, D), jnp.float32), 0.099609375, 1.8984375).astype(jnp.bfloat16),
        "qkv_weight": bell_draw(streams_of[9], (SECTIONS, D, QKV), D ** -0.5, 0.09375, ((0, 16), (2, 16))),
        "qkv_shrink": bell_draw(streams_of[10], (SECTIONS, D, RANKS), D ** -0.5, 0.09375, ((0, 16), (2, 16))),
        "qkv_expand": bell_draw(streams_of[11], (SECTIONS, RANKS, QKV), 128 ** -0.5, 0.5, ((0, 16), (2, 16))),
    }


adapter_alpha_scale = 32.0

def table_lookup(table, tenants):
    chosen = tenants[:, None] == jnp.arange(TENANTS, dtype=jnp.int32)[None, :]
    return lax.optimization_barrier(jnp.sum(jnp.where(chosen, table[None, :], 0), axis=1)).astype(jnp.int32)

def adapter_scale(tenants, adapter_rank, adapter_offset, first_col, col_count):
    lower = table_lookup(adapter_offset, tenants)
    tenant_ranks = table_lookup(adapter_rank, tenants)
    columns = first_col + jnp.arange(col_count, dtype=jnp.int32)
    inside = (columns[None, :] >= lower[:, None]) & (columns[None, :] < (lower + tenant_ranks)[:, None])
    scaling_factor = adapter_alpha_scale / tenant_ranks.astype(jnp.float32)
    return jnp.where(inside, scaling_factor[:, None], jnp.float32(0.0))

def rounded(values):
    return lax.optimization_barrier(values.astype(jnp.bfloat16)).astype(jnp.float32)

def reference(hidden, down_weight, down_shrink, down_up_factors, residual, tenant_ids, adapter_rank, adapter_offset, norm_gain, qkv_weight, qkv_shrink, qkv_expand):
    hidden_state = hidden.reshape(SECTIONS, ROWS, FF)
    resid_st = residual.reshape(SECTIONS, ROWS, D)
    tenant_st = tenant_ids.reshape(SECTIONS, ROWS)
    block = FF // N_TENSOR

    def down_section(items):
        acts, weight, shrink, expand, resid, tenants = items

        def add_block(carry, index):
            base_acc, low_acc = carry
            start = (index * block).astype(jnp.int32)
            part_acts = lax.dynamic_slice_in_dim(acts, start, block, 1)
            part_weight = lax.dynamic_slice_in_dim(weight, start, block, 0)
            part_shrink = lax.dynamic_slice_in_dim(shrink, start, block, 0)
            base_acc = base_acc + rounded(jnp.dot(part_acts, part_weight, preferred_element_type=jnp.float32))
            low_acc = low_acc + rounded(jnp.dot(part_acts, part_shrink, preferred_element_type=jnp.float32))
            return ((base_acc, low_acc), None)
        start_carry = (jnp.zeros((ROWS, D), jnp.float32), jnp.zeros((ROWS, RANKS), jnp.float32))
        (base, low_sum), unused = lax.scan(add_block, start_carry, jnp.arange(N_TENSOR, dtype=jnp.int32))
        small = (low_sum * adapter_scale(tenants, adapter_rank, adapter_offset, 0, RANKS)).astype(jnp.bfloat16)
        output = base + jnp.dot(small, expand, preferred_element_type=jnp.float32)
        return (resid.astype(jnp.float32) + output).astype(jnp.bfloat16)
    stream = lax.map(down_section, (hidden_state, down_weight, down_shrink, down_up_factors, resid_st, tenant_st))
    arrived = jnp.roll(stream, 1, axis=0)
    arrived_ids = jnp.roll(tenant_st, 1, axis=0)

    def qkv_section(items):
        rows_in, tenants, gain, weight, shrink, expand = items
        values = rows_in.astype(jnp.float32)
        inverse = lax.rsqrt(lax.optimization_barrier(jnp.mean(values * values, axis=-1, keepdims=True)) + 1e-05)
        normed = (values * inverse * gain.astype(jnp.float32)[None, :]).astype(jnp.bfloat16)
        shrunk = jnp.dot(normed, shrink, preferred_element_type=jnp.float32)
        small = (shrunk * adapter_scale(tenants, adapter_rank, adapter_offset, 0, RANKS)).astype(jnp.bfloat16)
        output = jnp.dot(normed, weight, preferred_element_type=jnp.float32) + jnp.dot(small, expand, preferred_element_type=jnp.float32)
        return output.astype(jnp.bfloat16)
    qkv = lax.map(qkv_section, (arrived, arrived_ids, norm_gain, qkv_weight, qkv_shrink, qkv_expand))
    return (stream.reshape(TOTAL_ROWS, D), qkv.reshape(TOTAL_ROWS, QKV))
```

```python
import jax
import jax.numpy as jnp
from jax import lax
from jax.sharding import PartitionSpec as P

adapter_alpha_scale = 32.0
BF = jnp.bfloat16
F32 = jnp.float32
NZ = 4
NY = 4
CHUNKS = 2


def send(block, dz=0, dy=0, ds=0):
    sections = lax.axis_size("section")
    group = NZ * NY
    route = []
    for s in range(sections):
        for z in range(NZ):
            for y in range(NY):
                to = ((s + ds) % sections) * group + ((z + dz) % NZ) * NY + (y + dy) % NY
                route.append((s * group + z * NY + y, to))
    return lax.ppermute(block, ("section", "tensor"), route)


def after(block, done):
    return lax.optimization_barrier((block, done))[0]


def table_lookup(table, tenants):
    chosen = tenants[:, None] == jnp.arange(table.shape[0], dtype=jnp.int32)[None, :]
    return jnp.sum(jnp.where(chosen, table[None, :], 0), axis=1)


def adapter_scale(tenants, adapter_rank, adapter_offset, col_count):
    lower = table_lookup(adapter_offset, tenants)
    tenant_ranks = table_lookup(adapter_rank, tenants)
    columns = jnp.arange(col_count, dtype=jnp.int32)
    inside = (columns[None, :] >= lower[:, None]) & (
        columns[None, :] < (lower + tenant_ranks)[:, None]
    )
    scaling_factor = adapter_alpha_scale / tenant_ranks.astype(F32)
    return jnp.where(inside, scaling_factor[:, None], F32(0.0))


def rolled(block, start, axis):
    size = block.shape[axis]
    return lax.dynamic_slice_in_dim(jnp.concatenate([block, block], axis), start, size, axis)


def dot(a, b):
    return jnp.dot(a, b, preferred_element_type=F32)


def per_device(
    hidden,
    down_weight,
    down_shrink,
    down_up_factors,
    residual,
    tenant_ids,
    adapter_rank,
    adapter_offset,
    norm_gain,
    qkv_weight,
    qkv_shrink,
    qkv_expand,
):
    my_index = lax.axis_index("tensor")
    z, y = my_index // NY, my_index % NY
    rows, ff = hidden.shape
    share = rows // (NZ * NY)
    width = down_weight.shape[2]
    ranks = down_shrink.shape[2]
    band = NZ * share
    step = width // CHUNKS
    half = step // 2
    own_cols = width // NZ

    shrink_full = lax.all_gather(qkv_shrink[0], "tensor", axis=1, tiled=True)
    gain = norm_gain[0].astype(F32)[:, None]
    arrived_ids = send(tenant_ids, 0, 0, 1)

    by_place = hidden.reshape(NZ, NY, share, ff)
    acts = [
        lax.dynamic_slice_in_dim(by_place, (y + d) % NY, 1, 1).reshape(band, ff) for d in range(NY)
    ]

    low = [dot(acts[d], down_shrink[0]) for d in range(NY)]
    up_own = down_up_factors[0]
    low_in = [send(low[d].astype(BF), 0, d) for d in (1, 2, 3)]
    low_y = low[0] + sum(part.astype(F32) for part in low_in)
    low_out = low_y.astype(BF)
    low_sum = low_y + sum(send(low_out, e, 0).astype(F32) for e in (1, 2, 3))
    my_ids = lax.dynamic_slice_in_dim(tenant_ids.reshape(NZ, NY, share), y, 1, 1).reshape(band)
    low_rows = (low_sum * adapter_scale(my_ids, adapter_rank, adapter_offset, ranks)).astype(BF)
    ups = [up_own] + [send(up_own, 0, NY - d) for d in (1, 2, 3)]
    up_part = jnp.concatenate([dot(low_rows, up) for up in ups], axis=1)
    up_part = rolled(up_part.reshape(band, NY, own_cols // NY), (NY - y) % NY, 1).reshape(
        band, own_cols
    )

    def down_parts(c):
        weight = down_weight[0][:, c * step : (c + 1) * step]
        return {d: dot(acts[d], weight).astype(BF) for d in (2, 1, 3, 0)}

    def reduce_y(parts):
        far_right = send(parts[2][:, :half], 0, 1)
        far_left = send(parts[2][:, half:], 0, NY - 1)
        right = jnp.concatenate(
            [
                (parts[1][:, :half].astype(F32) + far_right.astype(F32)).astype(BF),
                parts[1][:, half:],
            ],
            axis=1,
        )
        left = jnp.concatenate(
            [
                parts[3][:, :half],
                (parts[3][:, half:].astype(F32) + far_left.astype(F32)).astype(BF),
            ],
            axis=1,
        )
        from_left = send(right, 0, 1)
        from_right = send(left, 0, NY - 1)
        return parts[0].astype(F32), from_left, from_right

    def with_adapter(total, c):
        pieces = []
        per = step // own_cols
        for b in range(per):
            block = total[:, b * own_cols : (b + 1) * own_cols]
            pieces.append(block + jnp.where(z == c * per + b, up_part, F32(0.0)))
        return jnp.concatenate(pieces, axis=1)

    def reduce_z(total):
        pieces = [
            lax.dynamic_slice_in_dim(total, ((z + e) % NZ) * share, share, 0) for e in range(NZ)
        ]
        received = [send(pieces[e].astype(BF), e, 0) for e in (1, 2, 3)]
        return pieces[0], received

    def pass_on(block):
        return jnp.concatenate([send(block, e, 0, 1) for e in range(NZ)], axis=0)

    stream = []
    arrived = []
    order = None
    for c in range(CHUNKS):
        parts = down_parts(c)
        if order is not None:
            parts[2] = after(parts[2], order)
        own, from_left, from_right = reduce_y(parts)
        order = (from_left, from_right)
        total = own + from_left.astype(F32) + from_right.astype(F32)
        mine, received = reduce_z(with_adapter(total, c))
        block = residual[:, c * step : (c + 1) * step].astype(F32) + mine
        for part in received:
            block = block + part.astype(F32)
        block = block.astype(BF)
        stream.append(block)
        arrived.append(pass_on(block))

    qkv_matrix = jnp.concatenate([qkv_weight[0], shrink_full], axis=1)
    qkv_matrix = (qkv_matrix.astype(F32) * gain).astype(BF)

    sums = [F32(0.0)] * NY
    squares = [F32(0.0)] * NY
    for c in range(CHUNKS):
        block = arrived[c]
        block = after(block, order)
        matrix = qkv_matrix[c * step : (c + 1) * step]
        from_left = send(block, 0, 1)
        from_right = send(block, 0, NY - 1)
        far_a = send(from_left[:, :half], 0, 1)
        far_b = send(from_right[:, half:], 0, NY - 1)
        order = (far_a, far_b)
        for d, have in ((0, block), (1, from_right), (3, from_left)):
            sums[d] = sums[d] + dot(have, matrix)
            squares[d] = squares[d] + jnp.sum(have.astype(F32) ** 2, axis=1)
        sums[2] = sums[2] + dot(far_a, matrix[:half]) + dot(far_b, matrix[half:])
        squares[2] = (
            squares[2]
            + jnp.sum(far_a.astype(F32) ** 2, axis=1)
            + jnp.sum(far_b.astype(F32) ** 2, axis=1)
        )

    ids = rolled(rolled(arrived_ids.reshape(NZ, NY, share)[::-1], (NZ - 1 - z) % NZ, 0), y, 1)
    ids = ids.transpose(1, 0, 2).reshape(rows)
    product = jnp.concatenate(sums, axis=0)
    inverse = lax.rsqrt(jnp.concatenate(squares, axis=0) / width + 1e-05)[:, None]
    product = product * inverse
    cols = qkv_weight.shape[2]
    small = (
        product[:, cols:] * adapter_scale(ids, adapter_rank, adapter_offset, ranks)
    ).astype(BF)
    out = (product[:, :cols] + dot(small, qkv_expand[0])).astype(BF)
    out = out.reshape(NY, NZ, share, cols)
    out = rolled(rolled(out[:, ::-1], (NZ - 1 - z) % NZ, 1), (NY - y) % NY, 0)
    out = out.transpose(1, 0, 2, 3).reshape(rows, cols)
    return jnp.concatenate(stream, axis=1), out


def solution(mesh):
    in_specs = (
        P("section", "tensor"),
        P("section", "tensor", None),
        P("section", "tensor", None),
        P("section", None, "tensor"),
        P(("section", "tensor"), None),
        P("section"),
        P(),
        P(),
        P("section", None),
        P("section", None, "tensor"),
        P("section", None, "tensor"),
        P("section", None, "tensor"),
    )
    out_specs = (P(("section", "tensor"), None), P("section", "tensor"))
    return jax.shard_map(
        per_device, mesh=mesh, in_specs=in_specs, out_specs=out_specs, check_vma=False
    )
```

```python
import functools

import jax
import jax.numpy as jnp
from jax import lax
from jax.experimental import pallas as pl
from jax.experimental.pallas import tpu as pltpu
from jax.sharding import PartitionSpec as P

adapter_alpha_scale = 32.0
BF = jnp.bfloat16
F32 = jnp.float32
NZ = 4
NY = 4
FIRST = 1024
PIECES = 3


def send(block, dz=0, dy=0, ds=0):
    sections = lax.axis_size("section")
    group = NZ * NY
    route = []
    for s in range(sections):
        for z in range(NZ):
            for y in range(NY):
                to = ((s + ds) % sections) * group + ((z + dz) % NZ) * NY + (y + dy) % NY
                route.append((s * group + z * NY + y, to))
    return lax.ppermute(block, ("section", "tensor"), route)


def after(block, done):
    return lax.optimization_barrier((block, done))[0]


def table_lookup(table, tenants):
    chosen = tenants[:, None] == jnp.arange(table.shape[0], dtype=jnp.int32)[None, :]
    return jnp.sum(jnp.where(chosen, table[None, :], 0), axis=1)


def adapter_scale(tenants, adapter_rank, adapter_offset, columns):
    lower = table_lookup(adapter_offset, tenants)
    tenant_ranks = table_lookup(adapter_rank, tenants)
    inside = (columns[None, :] >= lower[:, None]) & (
        columns[None, :] < (lower + tenant_ranks)[:, None]
    )
    scaling_factor = adapter_alpha_scale / tenant_ranks.astype(F32)
    return jnp.where(inside, scaling_factor[:, None], F32(0.0))


def rolled(block, start, axis):
    size = block.shape[axis]
    return lax.dynamic_slice_in_dim(jnp.concatenate([block, block], axis), start, size, axis)


def dot(a, b):
    return jnp.dot(a, b, preferred_element_type=F32)


def rows_times(block, matrix):
    return lax.dot_general(
        block, matrix, (((1,), (1,)), ((), ())), preferred_element_type=F32
    )


def square_sums(block):
    values = block.astype(F32)
    return jnp.sum(values * values, axis=1, keepdims=True)


def staged_call(body, place, inputs, outputs, scratch, flops):
    n_in, n_out = len(inputs), len(outputs)

    def kernel(place, *refs):
        sources, targets = refs[:n_in], refs[n_in : n_in + n_out]
        held, made = refs[n_in + n_out : 2 * n_in + n_out], refs[2 * n_in + n_out : -2]
        in_sem, out_sem = refs[-2:]
        loads = [
            pltpu.make_async_copy(sources[i], held[i], in_sem.at[i]) for i in range(n_in)
        ]
        stores = [
            pltpu.make_async_copy(made[i], targets[i], out_sem.at[i]) for i in range(n_out)
        ]
        for load in loads:
            load.start()

        def ready(i):
            loads[i].wait()
            return held[i]

        def emit(i, value):
            made[i][...] = value
            stores[i].start()

        body(place, ready, emit, made[n_out:])
        for store in stores:
            store.wait()

    hbm = pl.BlockSpec(memory_space=pltpu.MemorySpace.HBM)
    return pl.pallas_call(
        kernel,
        in_specs=[pl.BlockSpec(memory_space=pltpu.MemorySpace.SMEM)] + [hbm] * n_in,
        out_specs=[hbm] * n_out,
        out_shape=outputs,
        scratch_shapes=[pltpu.VMEM(a.shape, a.dtype) for a in list(inputs) + list(outputs)]
        + scratch
        + [pltpu.SemaphoreType.DMA((n_in,)), pltpu.SemaphoreType.DMA((n_out,))],
        compiler_params=pltpu.CompilerParams(vmem_limit_bytes=58 << 20),
        cost_estimate=pl.CostEstimate(flops=flops, bytes_accessed=8 << 20, transcendentals=0),
    )(place, *inputs)


def pieces_of(weight, hidden, count):
    depth = weight.shape[0]
    cuts = [depth * k // (128 * count) * 128 for k in range(count)] + [depth]
    return list(zip(cuts[:-1], cuts[1:]))


def down_call(kernel, place, hidden, weight, outputs, scratch, more, flops):
    hbm = pl.BlockSpec(memory_space=pltpu.MemorySpace.HBM)
    rows, ff = hidden.shape
    return pl.pallas_call(
        kernel,
        in_specs=[pl.BlockSpec(memory_space=pltpu.MemorySpace.SMEM)] + [hbm] * (2 + len(more)),
        out_specs=[hbm] * len(outputs),
        out_shape=outputs,
        scratch_shapes=[
            pltpu.VMEM((rows, ff), BF),
            pltpu.VMEM((rows, ff), BF),
            pltpu.VMEM((ff, weight.shape[2]), BF),
            pltpu.SemaphoreType.DMA(()),
            pltpu.SemaphoreType.DMA((PIECES,)),
            pltpu.SemaphoreType.DMA((len(outputs),)),
            *[pltpu.VMEM(a.shape, a.dtype) for a in outputs],
            *scratch,
        ],
        compiler_params=pltpu.CompilerParams(vmem_limit_bytes=58 << 20),
        cost_estimate=pl.CostEstimate(
            flops=flops, bytes_accessed=2 * (rows * ff + ff * weight.shape[2]), transcendentals=0
        ),
    )(place, hidden, weight, *more)


def weight_loads(weight, taps, sem):
    loads = []
    for k, (low, high) in enumerate(pieces_of(taps, None, PIECES)):
        rows = pl.ds(low, high - low)
        loads.append(
            pltpu.make_async_copy(weight.at[0, rows, :], taps.at[rows, :], sem.at[k])
        )
    return loads


def reordered(place, raw, acts, share, distances):
    for i, d in enumerate(distances):
        y_at = lax.rem(place[1] + d, NY)
        for zz in range(NZ):
            start = pl.multiple_of((zz * NY + y_at) * share, share)
            k = i * NZ + zz
            acts[k * share : (k + 1) * share, :] = raw[pl.ds(start, share), :]


def far_kernel(
    share, place, hidden, weight, shrink, far_a, far_b, low, low_1, low_2, low_3, raw, acts, taps,
    raw_sem, taps_sem, out_sem, *rest
):
    made, (acc, shrink_in, shrink_sem) = rest[:6], rest[6:]
    band = NZ * share
    half = taps.shape[1] // 2
    load = pltpu.make_async_copy(hidden, raw, raw_sem)
    small = pltpu.make_async_copy(shrink.at[0], shrink_in, shrink_sem)
    loads = weight_loads(weight, taps, taps_sem)
    stores = [
        pltpu.make_async_copy(made[i], target, out_sem.at[i])
        for i, target in enumerate((far_a, far_b, low, low_1, low_2, low_3))
    ]
    for copy in [load, small, *loads]:
        copy.start()
    load.wait()
    reordered(place, raw, acts, share, (0, 1, 2, 3))
    small.wait()
    part = dot(acts[...], shrink_in[...])
    for d in range(NY):
        made[2 + d][...] = part[d * band : (d + 1) * band].astype(made[2 + d].dtype)
        stores[2 + d].start()
    cuts = pieces_of(taps, None, PIECES)
    for k, (first, last) in enumerate(cuts):
        loads[k].wait()
        part = dot(acts[2 * band : 3 * band, first:last], taps[first:last, :])
        if k > 0:
            part = acc[...] + part
        if k < len(cuts) - 1:
            acc[...] = part
        else:
            made[0][...] = part[:, :half].astype(BF)
            stores[0].start()
            made[1][...] = part[:, half:].astype(BF)
            stores[1].start()
    for store in stores:
        store.wait()


def far_products(place, hidden, weight, shrink, share):
    rows, ff = hidden.shape
    width, ranks = weight.shape[2], shrink.shape[2]
    band = NZ * share
    outputs = [jax.ShapeDtypeStruct((band, width // 2), BF)] * 2
    outputs += [jax.ShapeDtypeStruct((band, ranks), F32)]
    outputs += [jax.ShapeDtypeStruct((band, ranks), BF)] * 3
    scratch = [
        pltpu.VMEM((band, width), F32),
        pltpu.VMEM((ff, ranks), BF),
        pltpu.SemaphoreType.DMA(()),
    ]
    return down_call(
        functools.partial(far_kernel, share), place, hidden, weight, outputs, scratch, [shrink],
        2 * ff * (band * width + rows * ranks),
    )


def rest_kernel(
    share, place, hidden, weight, own, right, left, raw, acts, taps, raw_sem, taps_sem, out_sem,
    own_made, right_made, left_made, acc
):
    band = NZ * share
    load = pltpu.make_async_copy(hidden, raw, raw_sem)
    loads = weight_loads(weight, taps, taps_sem)
    made = (right_made, left_made, own_made)
    stores = [
        pltpu.make_async_copy(made[i], target, out_sem.at[i])
        for i, target in enumerate((right, left, own))
    ]
    for copy in [load, *loads]:
        copy.start()
    load.wait()
    reordered(place, raw, acts, share, (1, 3, 0))
    cuts = pieces_of(taps, None, PIECES)
    for k, (first, last) in enumerate(cuts):
        loads[k].wait()
        for i in range(3):
            rows = slice(i * band, (i + 1) * band)
            part = dot(acts[rows, first:last], taps[first:last, :])
            if k > 0:
                part = acc[rows, :] + part
            if k < len(cuts) - 1:
                acc[rows, :] = part
            else:
                made[i][...] = part.astype(BF)
                stores[i].start()
    for store in stores:
        store.wait()


def rest_products(place, hidden, weight, share):
    rows, ff = hidden.shape
    width = weight.shape[2]
    band = NZ * share
    return down_call(
        functools.partial(rest_kernel, share), place, hidden, weight,
        [jax.ShapeDtypeStruct((band, width), BF)] * 3,
        [pltpu.VMEM((3 * band, width), F32)], [], 6 * band * ff * width,
    )


def fold(place, right, left, in_a, in_b):
    half = in_a.shape[1]

    def body(place, ready, emit, scratch):
        base, more = ready(0), ready(2)
        emit(
            0,
            jnp.concatenate(
                [(base[:, :half].astype(F32) + more[...].astype(F32)).astype(BF), base[:, half:]],
                axis=1,
            ),
        )
        base, more = ready(1), ready(3)
        emit(
            1,
            jnp.concatenate(
                [base[:, :half], (base[:, half:].astype(F32) + more[...].astype(F32)).astype(BF)],
                axis=1,
            ),
        )

    outputs = [jax.ShapeDtypeStruct(right.shape, BF)] * 2
    return staged_call(body, place, (right, left, in_a, in_b), outputs, [], right.size)


def totals(share, place, parts, low, scale, ups):
    band, width = parts[0].shape
    tile = ups[0].shape[1]

    def body(place, ready, emit, scratch):
        (total,) = scratch
        low_sum = ready(0)[...]
        for i in (1, 2, 3):
            low_sum = low_sum + ready(i)[...].astype(F32)
        rows = (low_sum * ready(4)[...]).astype(BF)
        added = [dot(rows, ready(5 + d)[...]) for d in range(NY)]
        own, left, right = ready(9), ready(10), ready(11)
        total[...] = own[...].astype(F32) + left[...].astype(F32) + right[...].astype(F32)
        for d in range(NY):
            at = (place[0] * NY + lax.rem(place[1] + NY - d, NY)) * tile
            total[:, pl.ds(pl.multiple_of(at, tile), tile)] += added[d]
        for e in (2, 1, 3, 0):
            at = pl.multiple_of(lax.rem(place[0] + e, NZ) * share, share)
            emit(e, total[pl.ds(at, share), :].astype(F32 if e == 0 else BF))

    outputs = [jax.ShapeDtypeStruct((share, width), F32)]
    outputs += [jax.ShapeDtypeStruct((share, width), BF)] * 3
    return staged_call(
        body, place, (*low, scale, *ups, *parts), outputs, [pltpu.VMEM((band, width), F32)],
        2 * band * width * 128,
    )


def near_products(place, blocks, matrix):
    rows, cols = blocks[0].shape[0], matrix.shape[0]
    count = len(blocks)

    def body(place, ready, emit, scratch):
        taps = ready(0)
        for i in range(count):
            block = ready(1 + i)
            emit(2 * i, rows_times(block[...], taps[...]))
            emit(2 * i + 1, square_sums(block[...]))

    outputs = [jax.ShapeDtypeStruct((rows, cols), F32), jax.ShapeDtypeStruct((rows, 1), F32)]
    flops = 2 * count * rows * cols * matrix.shape[1]
    return staged_call(body, place, (matrix, *blocks), outputs * count, [], flops)


def output_products(share, width, place, *args):
    gathered, far_a, matrix_0, expand = args[0], args[2], args[1], args[-1]
    rows, both, cols = gathered.shape[0], matrix_0.shape[0], expand.shape[0]
    half = far_a.shape[1]

    def body(place, ready, emit, scratch):
        acc, sq = scratch
        block, taps = ready(0), ready(1)
        acc[...] = rows_times(block[...], taps[...])
        sq[...] = square_sums(block[...])
        far_a, far_b, taps = ready(2), ready(3), ready(4)
        far = rows_times(far_a[...], taps[:, :half]) + rows_times(far_b[...], taps[:, half:])
        far_sq = square_sums(far_a[...]) + square_sums(far_b[...])
        blocks = ((0, ready(5)[...], ready(6)[...]), (1, ready(7)[...], ready(8)[...]))
        blocks += ((2, far, far_sq), (3, ready(9)[...], ready(10)[...]))
        for d, part, part_sq in blocks:
            y_at = lax.rem(place[1] + d, NY)
            for e in range(NZ):
                z_at = lax.rem(place[0] + NZ - e, NZ)
                at = pl.ds(pl.multiple_of((z_at * NY + y_at) * share, share), share)
                acc[at, :] += part[e * share : (e + 1) * share]
                sq[at, :] += part_sq[e * share : (e + 1) * share]
        inverse = lax.rsqrt(sq[...] / width + 1e-05)
        scale, expand = ready(11), ready(12)
        small = (acc[:, cols:] * inverse * scale[...]).astype(BF)
        result = acc[:, :cols] * inverse + rows_times(small, expand[...])
        emit(0, result.T.astype(BF))

    return staged_call(
        body,
        place,
        args,
        [jax.ShapeDtypeStruct((cols, rows), BF)],
        [pltpu.VMEM((rows, both), F32), pltpu.VMEM((rows, 1), F32)],
        2 * rows * both * 2048,
    )[0]


def per_device(
    hidden,
    down_weight,
    down_shrink,
    down_up_factors,
    residual,
    tenant_ids,
    adapter_rank,
    adapter_offset,
    norm_gain,
    qkv_weight,
    qkv_shrink,
    qkv_expand,
):
    my_index = lax.axis_index("tensor")
    z, y = my_index // NY, my_index % NY
    rows, ff = hidden.shape
    share = rows // (NZ * NY)
    width = down_weight.shape[2]
    ranks = down_shrink.shape[2]
    band = NZ * share
    z_groups = [[zz * NY + yy for zz in range(NZ)] for yy in range(NY)]
    fence = lax.optimization_barrier
    place = jnp.stack([z, y]).astype(jnp.int32)

    shrink_own = qkv_shrink[0].T
    shrink_z = lax.all_gather(
        jnp.concatenate([shrink_own, shrink_own], axis=0)[None],
        "tensor", axis=0, tiled=True, axis_index_groups=z_groups,
    )
    up_own = down_up_factors[0]
    ups = [up_own] + [send(up_own, 0, d) for d in (1, 2, 3)]

    far_a, far_b, low_own, *low_parts = far_products(
        place, hidden, down_weight, down_shrink, share
    )
    in_a, in_b = send(far_a, 0, 1), send(far_b, 0, NY - 1)
    low_in = [send(low_parts[d - 1], 0, d) for d in (1, 2, 3)]
    own, right, left = rest_products(place, after(hidden, (far_a, ups)), down_weight, share)
    my_ids = lax.dynamic_slice_in_dim(tenant_ids.reshape(NZ, NY, share), y, 1, 1).reshape(band)
    my_scale = adapter_scale(my_ids, adapter_rank, adapter_offset, jnp.arange(ranks))
    in_a, in_b, low_in, own, right, left, my_scale = fence(
        (in_a, in_b, low_in, own, right, left, my_scale)
    )

    right, left = fold(place, right, left, in_a, in_b)
    from_left, from_right = send(right, 0, 1), send(left, 0, NY - 1)
    low_y = low_own + sum(part.astype(F32) for part in low_in)
    low_out = low_y.astype(BF)
    low = [low_y] + [send(low_out, e, 0) for e in (2, 1, 3)]
    per = ranks // (NZ * NY)
    numbers = rolled(jnp.arange(ranks).reshape(NZ, NY, per), y, 1)
    numbers = numbers.transpose(1, 0, 2).reshape(ranks)
    expand = rolled(qkv_expand[0].reshape(NZ, NY, per, -1), y, 1)
    expand = expand.transpose(1, 0, 2, 3).reshape(ranks, -1).T
    from_left, from_right, low, my_scale, own, expand, numbers = fence(
        (from_left, from_right, low, my_scale, own, expand, numbers)
    )
    shrink_z = after(shrink_z, low)[:, :per].reshape(-1, width)

    pieces = totals(share, place, (own, from_left, from_right), low, my_scale, ups)
    swapped = [send(pieces[e], e, 0) for e in (2, 1, 3)]
    shrink_left, shrink_right = send(shrink_z, 0, 1), send(shrink_z, 0, NY - 1)
    swapped, shrink_left, shrink_right, tenant_ids, shrink_z = fence(
        (swapped, shrink_left, shrink_right, tenant_ids, shrink_z)
    )
    block = residual.astype(F32) + pieces[0]
    for part in swapped:
        block = block + part.astype(F32)
    stream = block.astype(BF)

    arrived = send(stream[:, :FIRST], 0, 0, 1)
    arrived_ids = send(tenant_ids, 0, 0, 1)
    cut = shrink_z.shape[0] // 2
    shrink_far = [send(shrink_left[:cut], 0, 1), send(shrink_right[cut:], 0, NY - 1)]
    stream, arrived = fence((stream, arrived))
    gathered = lax.all_gather(arrived, "tensor", axis=0, tiled=True)
    passed = [send(stream[:, FIRST:], e, 0, 1) for e in (2, 1, 3, 0)]
    passed, arrived_ids, shrink_far = fence((passed, arrived_ids, shrink_far))
    matrix = jnp.concatenate(
        [qkv_weight[0].T, shrink_z, shrink_right, *shrink_far, shrink_left], axis=0
    )
    matrix = (matrix.astype(F32) * norm_gain[0].astype(F32)[None, :]).astype(BF)
    matrix_0, matrix_1 = matrix[:, :FIRST], matrix[:, FIRST:]
    scale = adapter_scale(arrived_ids, adapter_rank, adapter_offset, numbers)
    block = jnp.concatenate([passed[3], passed[1], passed[0], passed[2]], axis=0)

    half = (width - FIRST) // 2
    from_left, from_right = send(block, 0, 1), send(block, 0, NY - 1)
    near = near_products(place, (block,), matrix_1)
    from_left, from_right, near, scale, matrix_0 = fence(
        (from_left, from_right, near, scale, matrix_0)
    )
    far_a = send(from_left[:, :half], 0, 1)
    far_b = send(from_right[:, half:], 0, NY - 1)
    near = [*near, *near_products(place, (from_right, from_left), matrix_1)]
    far_a, far_b, near = fence((far_a, far_b, near))
    out = output_products(
        share, width, place, gathered, matrix_0, far_a, far_b, matrix_1, *near, scale,
        expand,
    )
    return stream, out.T


def solution(mesh):
    in_specs = (
        P("section", "tensor"),
        P("section", "tensor", None),
        P("section", "tensor", None),
        P("section", None, "tensor"),
        P(("section", "tensor"), None),
        P("section"),
        P(),
        P(),
        P("section", None),
        P("section", None, "tensor"),
        P("section", None, "tensor"),
        P("section", None, "tensor"),
    )
    out_specs = (P(("section", "tensor"), None), P("section", "tensor"))
    return jax.shard_map(
        per_device, mesh=mesh, in_specs=in_specs, out_specs=out_specs, check_vma=False
    )
```

```python
import functools

import jax
import jax.numpy as jnp
from jax import lax
from jax.experimental import pallas as pl
from jax.experimental.pallas import tpu as pltpu
from jax.sharding import PartitionSpec as P

adapter_alpha_scale = 32.0
BF = jnp.bfloat16
F32 = jnp.float32
NZ = 4
NY = 4
PIECES = 2
VMEM_BYTES = 40 << 20


def send(block, dz=0, dy=0, ds=0):
    sections = lax.axis_size("section")
    group = NZ * NY
    route = []
    for s in range(sections):
        for z in range(NZ):
            for y in range(NY):
                to = ((s + ds) % sections) * group + ((z + dz) % NZ) * NY + (y + dy) % NY
                route.append((s * group + z * NY + y, to))
    return lax.ppermute(block, ("section", "tensor"), route)


def after(block, done):
    return lax.optimization_barrier((block, done))[0]


def table_lookup(table, tenants):
    chosen = tenants[:, None] == jnp.arange(table.shape[0], dtype=jnp.int32)[None, :]
    return jnp.sum(jnp.where(chosen, table[None, :], 0), axis=1)


def adapter_scale(tenants, adapter_rank, adapter_offset, columns):
    lower = table_lookup(adapter_offset, tenants)
    tenant_ranks = table_lookup(adapter_rank, tenants)
    inside = (columns[None, :] >= lower[:, None]) & (
        columns[None, :] < (lower + tenant_ranks)[:, None]
    )
    scaling_factor = adapter_alpha_scale / tenant_ranks.astype(F32)
    return jnp.where(inside, scaling_factor[:, None], F32(0.0))


def dot(a, b):
    return jnp.dot(a, b, preferred_element_type=F32)


def rows_times(block, matrix):
    return lax.dot_general(
        block, matrix, (((1,), (1,)), ((), ())), preferred_element_type=F32
    )


def staged_call(body, place, inputs, outputs, scratch, flops):
    n_in, n_out = len(inputs), len(outputs)

    def kernel(place, *refs):
        sources, targets = refs[:n_in], refs[n_in : n_in + n_out]
        held, made = refs[n_in + n_out : 2 * n_in + n_out], refs[2 * n_in + n_out : -2]
        in_sem, out_sem = refs[-2:]
        loads = [
            pltpu.make_async_copy(sources[i], held[i], in_sem.at[i]) for i in range(n_in)
        ]
        stores = [
            pltpu.make_async_copy(made[i], targets[i], out_sem.at[i]) for i in range(n_out)
        ]
        for load in loads:
            load.start()

        def ready(i):
            loads[i].wait()
            return held[i]

        def emit(i, value):
            made[i][...] = value
            stores[i].start()

        body(place, ready, emit, made[n_out:])
        for store in stores:
            store.wait()

    hbm = pl.BlockSpec(memory_space=pltpu.MemorySpace.HBM)
    return pl.pallas_call(
        kernel,
        in_specs=[pl.BlockSpec(memory_space=pltpu.MemorySpace.SMEM)] + [hbm] * n_in,
        out_specs=[hbm] * n_out,
        out_shape=outputs,
        scratch_shapes=[pltpu.VMEM(a.shape, a.dtype) for a in list(inputs) + list(outputs)]
        + scratch
        + [pltpu.SemaphoreType.DMA((n_in,)), pltpu.SemaphoreType.DMA((n_out,))],
        compiler_params=pltpu.CompilerParams(vmem_limit_bytes=VMEM_BYTES),
        cost_estimate=pl.CostEstimate(flops=flops, bytes_accessed=8 << 20, transcendentals=0),
    )(place, *inputs)


def pieces_of(weight, hidden, count):
    depth = weight.shape[0]
    cuts = [depth * k // (128 * count) * 128 for k in range(count)] + [depth]
    return list(zip(cuts[:-1], cuts[1:]))


def down_call(kernel, place, hidden, weight, outputs, scratch, more, flops):
    hbm = pl.BlockSpec(memory_space=pltpu.MemorySpace.HBM)
    rows, ff = hidden.shape
    return pl.pallas_call(
        kernel,
        in_specs=[pl.BlockSpec(memory_space=pltpu.MemorySpace.SMEM)] + [hbm] * (2 + len(more)),
        out_specs=[hbm] * len(outputs),
        out_shape=outputs,
        scratch_shapes=[
            pltpu.VMEM((rows, ff), BF),
            pltpu.VMEM((rows, ff), BF),
            pltpu.VMEM((ff, weight.shape[2]), BF),
            pltpu.SemaphoreType.DMA(()),
            pltpu.SemaphoreType.DMA((PIECES,)),
            pltpu.SemaphoreType.DMA((len(outputs),)),
            *[pltpu.VMEM(a.shape, a.dtype) for a in outputs],
            *scratch,
        ],
        compiler_params=pltpu.CompilerParams(vmem_limit_bytes=(58 << 20)),
        cost_estimate=pl.CostEstimate(
            flops=flops, bytes_accessed=2 * (rows * ff + ff * weight.shape[2]), transcendentals=0
        ),
    )(place, hidden, weight, *more)


def weight_loads(weight, taps, sem):
    loads = []
    for k, (low, high) in enumerate(pieces_of(taps, None, PIECES)):
        rows = pl.ds(low, high - low)
        loads.append(
            pltpu.make_async_copy(weight.at[0, rows, :], taps.at[rows, :], sem.at[k])
        )
    return loads


def reordered(place, raw, acts, share, distances):
    for i, d in enumerate(distances):
        y_at = lax.rem(place[1] + d, NY)
        for zz in range(NZ):
            start = pl.multiple_of((zz * NY + y_at) * share, share)
            k = i * NZ + zz
            acts[k * share : (k + 1) * share, :] = raw[pl.ds(start, share), :].astype(acts.dtype)


def far_kernel(
    share, place, hidden, weight, shrink, far_a, far_b, low, low_1, low_2, low_3, raw, acts, taps,
    raw_sem, taps_sem, out_sem, *rest
):
    made, (acc, low_all, shrink_in, shrink_sem) = rest[:6], rest[6:]
    band = NZ * share
    half = taps.shape[1] // 2
    load = pltpu.make_async_copy(hidden, raw, raw_sem)
    small = pltpu.make_async_copy(shrink.at[0], shrink_in, shrink_sem)
    loads = weight_loads(weight, taps, taps_sem)
    stores = [
        pltpu.make_async_copy(made[i], target, out_sem.at[i])
        for i, target in enumerate((far_a, far_b, low, low_1, low_2, low_3))
    ]
    for copy in [load, small, *loads]:
        copy.start()
    load.wait()
    reordered(place, raw, acts, share, (2,))
    small.wait()
    low_all[...] = dot(raw[...], shrink_in[...])
    for d in range(NY):
        reordered(place, low_all, made[2 + d], share, (d,))
        stores[2 + d].start()
    cuts = pieces_of(taps, None, PIECES)
    for k, (first, last) in enumerate(cuts):
        loads[k].wait()
        part = dot(acts[:band, first:last], taps[first:last, :])
        if k > 0:
            part = acc[...] + part
        if k < len(cuts) - 1:
            acc[...] = part
        else:
            made[0][...] = part[:, :half].astype(BF)
            stores[0].start()
            made[1][...] = part[:, half:].astype(BF)
            stores[1].start()
    for store in stores:
        store.wait()


def far_products(place, hidden, weight, shrink, share):
    rows, ff = hidden.shape
    width, ranks = weight.shape[2], shrink.shape[2]
    band = NZ * share
    outputs = [jax.ShapeDtypeStruct((band, width // 2), BF)] * 2
    outputs += [jax.ShapeDtypeStruct((band, ranks), F32)]
    outputs += [jax.ShapeDtypeStruct((band, ranks), BF)] * 3
    scratch = [
        pltpu.VMEM((band, width), F32),
        pltpu.VMEM((rows, ranks), F32),
        pltpu.VMEM((ff, ranks), BF),
        pltpu.SemaphoreType.DMA(()),
    ]
    return down_call(
        functools.partial(far_kernel, share), place, hidden, weight, outputs, scratch, [shrink],
        2 * ff * (band * width + rows * ranks),
    )


def rest_kernel(share, distances, place, hidden, weight, *refs):
    count = len(distances)
    targets, refs = refs[:count], refs[count:]
    raw, acts, taps, raw_sem, taps_sem, out_sem, *made = refs
    made, acc = made[:count], made[count]
    band = NZ * share
    load = pltpu.make_async_copy(hidden, raw, raw_sem)
    loads = weight_loads(weight, taps, taps_sem)
    stores = [pltpu.make_async_copy(made[i], targets[i], out_sem.at[i]) for i in range(count)]
    for copy in [load, *loads]:
        copy.start()
    load.wait()
    reordered(place, raw, acts, share, distances)
    cuts = pieces_of(taps, None, PIECES)
    for k, (first, last) in enumerate(cuts):
        loads[k].wait()
        for i in range(count):
            rows = slice(i * band, (i + 1) * band)
            part = dot(acts[rows, first:last], taps[first:last, :])
            if k > 0:
                part = acc[rows, :] + part
            if k < len(cuts) - 1:
                acc[rows, :] = part
            else:
                made[i][...] = part.astype(BF)
                stores[i].start()
    for store in stores:
        store.wait()


def rest_products(place, hidden, weight, share, distances):
    rows, ff = hidden.shape
    width = weight.shape[2]
    band = NZ * share
    count = len(distances)
    return down_call(
        functools.partial(rest_kernel, share, distances), place, hidden, weight,
        [jax.ShapeDtypeStruct((band, width), BF)] * count,
        [pltpu.VMEM((count * band, width), F32)], [], 2 * count * band * ff * width,
    )


def fold_kernel(right, left, in_a, in_b, right_out, left_out, base, more, sem, out_sem):
    half = in_a.shape[1]
    sides = ((right, in_a, right_out, 0), (left, in_b, left_out, half))
    loads, stores = [], []
    for i, (whole, arrived, target, first) in enumerate(sides):
        columns = pl.ds(first, half)
        loads.append(pltpu.make_async_copy(whole.at[:, columns], base.at[i], sem.at[2 * i]))
        loads.append(pltpu.make_async_copy(arrived, more.at[i], sem.at[2 * i + 1]))
        stores.append(pltpu.make_async_copy(base.at[i], target.at[:, columns], out_sem.at[i]))
    for load in loads:
        load.start()
    for i in range(2):
        loads[2 * i].wait()
        loads[2 * i + 1].wait()
        base[i] = (base[i].astype(F32) + more[i].astype(F32)).astype(BF)
        stores[i].start()
    for store in stores:
        store.wait()


def fold(right, left, in_a, in_b):
    hbm = pl.BlockSpec(memory_space=pltpu.MemorySpace.HBM)
    return pl.pallas_call(
        fold_kernel,
        in_specs=[hbm] * 4,
        out_specs=[hbm] * 2,
        out_shape=[jax.ShapeDtypeStruct(right.shape, BF)] * 2,
        input_output_aliases={0: 0, 1: 1},
        scratch_shapes=[
            pltpu.VMEM((2, *in_a.shape), BF),
            pltpu.VMEM((2, *in_a.shape), BF),
            pltpu.SemaphoreType.DMA((4,)),
            pltpu.SemaphoreType.DMA((2,)),
        ],
        compiler_params=pltpu.CompilerParams(vmem_limit_bytes=VMEM_BYTES),
        cost_estimate=pl.CostEstimate(
            flops=right.size, bytes_accessed=6 * right.size, transcendentals=0
        ),
    )(right, left, in_a, in_b)


def total_kernel(
    share, place, low, low_1, low_2, low_3, scale, up_0, up_1, up_2, up_3, own, left, right,
    out_0, out_1, out_2, out_3, low_in, more_in, scale_in, up_in, parts, added, total, piece_0,
    pieces, low_sem, part_sem, out_sem
):
    tile = up_0.shape[1]
    wide = NY * tile
    order = (2, 1, 3, 0)
    outs = (out_0, out_1, out_2, out_3)

    def rows_of(e):
        return pl.ds(pl.multiple_of(lax.rem(place[0] + e, NZ) * share, share), share)

    loads = [
        pltpu.make_async_copy(low, low_in, low_sem.at[0]),
        pltpu.make_async_copy(scale, scale_in, low_sem.at[1]),
    ]
    for i, source in enumerate((low_1, low_2, low_3)):
        loads.append(pltpu.make_async_copy(source, more_in.at[i], low_sem.at[2 + i]))
    for i, source in enumerate((up_0, up_1, up_2, up_3)):
        loads.append(
            pltpu.make_async_copy(
                source.at[pl.ds(0, low.shape[1]), :], up_in.at[i], low_sem.at[5 + i]
            )
        )
    part_loads = {
        e: [
            pltpu.make_async_copy(
                source.at[rows_of(e), :], parts.at[i, pl.ds(e * share, share), :], part_sem.at[e, i]
            )
            for i, source in enumerate((own, left, right))
        ]
        for e in order
    }
    stores = [
        pltpu.make_async_copy(
            piece_0 if e == 0 else pieces.at[e - 1], outs[e], out_sem.at[e]
        )
        for e in range(NZ)
    ]
    for load in loads:
        load.start()
    for e in order:
        for load in part_loads[e]:
            load.start()
    for load in loads:
        load.wait()
    low_sum = low_in[...]
    for i in range(3):
        low_sum = low_sum + more_in[i].astype(F32)
    rows = (low_sum * scale_in[...]).astype(BF)
    for d in range(NY):
        at = lax.rem(place[1] + NY - d, NY) * tile
        added[:, pl.ds(pl.multiple_of(at, tile), tile)] = dot(rows, up_in[d])
    columns = pl.ds(pl.multiple_of(place[0] * wide, wide), wide)
    for e in order:
        for load in part_loads[e]:
            load.wait()
        at = slice(e * share, (e + 1) * share)
        total[...] = (
            parts[0, at, :].astype(F32) + parts[1, at, :].astype(F32) + parts[2, at, :].astype(F32)
        )
        total[:, columns] += added[rows_of(e), :]
        if e == 0:
            piece_0[...] = total[...]
        else:
            pieces[e - 1] = total[...].astype(BF)
        stores[e].start()
    for store in stores:
        store.wait()


def totals(share, place, parts, low, scale, ups):
    band, width = parts[0].shape
    ranks, tile = low[0].shape[1], ups[0].shape[1]
    hbm = pl.BlockSpec(memory_space=pltpu.MemorySpace.HBM)
    return pl.pallas_call(
        functools.partial(total_kernel, share),
        in_specs=[pl.BlockSpec(memory_space=pltpu.MemorySpace.SMEM)] + [hbm] * 12,
        out_specs=[hbm] * 4,
        out_shape=[jax.ShapeDtypeStruct((share, width), F32)]
        + [jax.ShapeDtypeStruct((share, width), BF)] * 3,
        scratch_shapes=[
            pltpu.VMEM((band, ranks), F32),
            pltpu.VMEM((3, band, ranks), BF),
            pltpu.VMEM((band, ranks), F32),
            pltpu.VMEM((NY, ranks, tile), BF),
            pltpu.VMEM((3, band, width), BF),
            pltpu.VMEM((band, NY * tile), F32),
            pltpu.VMEM((share, width), F32),
            pltpu.VMEM((share, width), F32),
            pltpu.VMEM((3, share, width), BF),
            pltpu.SemaphoreType.DMA((9,)),
            pltpu.SemaphoreType.DMA((NZ, 3)),
            pltpu.SemaphoreType.DMA((NZ,)),
        ],
        compiler_params=pltpu.CompilerParams(vmem_limit_bytes=VMEM_BYTES),
        cost_estimate=pl.CostEstimate(
            flops=2 * band * width * 128, bytes_accessed=10 * band * width, transcendentals=0
        ),
    )(place, *low, scale, *ups, *parts)


def normalised(share, place, pieces, gain, factors, scale):
    width = pieces[0].shape[1]
    per = factors[0].shape[0]
    band = NZ * share

    def body(place, ready, emit, scratch):
        block, taps = scratch
        gain = ready(0)[...].astype(F32)
        for e in range(NZ):
            values = ready(1 + e)[...].astype(F32)
            mean = jnp.mean(values * values, axis=1, keepdims=True)
            at = pl.multiple_of(lax.rem(place[0] + NZ - e, NZ) * share, share)
            block[pl.ds(at, share), :] = (values * lax.rsqrt(mean + 1e-05) * gain).astype(BF)
        emit(0, block[...])
        for d in range(NY):
            at = pl.multiple_of(lax.rem(place[1] + NY - d, NY) * per, per)
            taps[pl.ds(at, per), :] = ready(1 + NZ + d)[...]
        emit(1, (rows_times(taps[...], block[...]) * ready(1 + NZ + NY)[...]).astype(BF))

    outputs = [
        jax.ShapeDtypeStruct((band, width), BF),
        jax.ShapeDtypeStruct((NY * per, band), BF),
    ]
    scratch = [pltpu.VMEM((band, width), BF), pltpu.VMEM((NY * per, width), BF)]
    return staged_call(
        body, place, (gain, *pieces, *factors, scale), outputs, scratch, 2 * band * width * 128
    )


def near_products(place, blocks, matrix):
    rows, cols = blocks[0].shape[0], matrix.shape[0]
    count = len(blocks)

    def body(place, ready, emit, scratch):
        taps = ready(0)
        for i in range(count):
            emit(i, rows_times(ready(1 + i)[...], taps[...]))

    outputs = [jax.ShapeDtypeStruct((rows, cols), F32)] * count
    flops = 2 * count * rows * cols * matrix.shape[1]
    return staged_call(body, place, (matrix, *blocks), outputs, [], flops)


def joined_products(share, place, right, left, matrix, own, small, expand):
    cols, ranks = matrix.shape[0], expand.shape[0]
    band = NZ * share
    wide = ranks // NZ

    def body(place, ready, emit, scratch):
        acc, factors = scratch
        held = ready(0)
        for e in range(NZ):
            at = pl.multiple_of(lax.rem(place[0] + NZ - e, NZ) * wide, wide)
            factors[e * wide : (e + 1) * wide, :] = held[pl.ds(at, wide), :]

        def put(d, part):
            put_rows(share, place, acc, d, part)

        def adapter(i):
            return lax.dot_general(
                ready(1 + i)[...], factors[...], (((0,), (0,)), ((), ())),
                preferred_element_type=F32,
            )

        put(2, adapter(2))
        put(0, ready(5)[...] + adapter(0))
        taps = ready(6)
        put(1, adapter(3) + rows_times(ready(7)[...], taps[...]))
        put(3, adapter(1) + rows_times(ready(8)[...], taps[...]))
        emit(0, acc[...])

    return staged_call(
        body,
        place,
        (expand, *small, own, matrix, right, left),
        [jax.ShapeDtypeStruct((NY * band, cols), F32)],
        [pltpu.VMEM((NY * band, cols), F32), pltpu.VMEM((ranks, cols), BF)],
        4 * band * cols * matrix.shape[1],
    )[0]


def put_rows(share, place, acc, d, part, add=False):
    y_at = lax.rem(place[1] + d, NY)
    for zz in range(NZ):
        at = pl.ds(pl.multiple_of((zz * NY + y_at) * share, share), share)
        rows = part[zz * share : (zz + 1) * share]
        acc[at, :] = acc[at, :] + rows if add else rows


def output_products(share, place, far_a, far_b, matrix, joined):
    rows, cols = joined.shape

    def body(place, ready, emit, scratch):
        taps = ready(0)
        part = jnp.concatenate(
            [rows_times(ready(1)[...], taps[...]), rows_times(ready(2)[...], taps[...])], axis=0
        )
        acc = ready(3)
        put_rows(share, place, acc, 2, part, True)
        emit(0, acc[...].T.astype(BF))

    return staged_call(
        body, place, (matrix, far_a, far_b, joined),
        [jax.ShapeDtypeStruct((cols, rows), BF)], [], 4 * far_a.size * cols,
    )[0]


def per_device(
    hidden,
    down_weight,
    down_shrink,
    down_up_factors,
    residual,
    tenant_ids,
    adapter_rank,
    adapter_offset,
    norm_gain,
    qkv_weight,
    qkv_shrink,
    qkv_expand,
):
    my_index = lax.axis_index("tensor")
    z, y = my_index // NY, my_index % NY
    rows, ff = hidden.shape
    share = rows // (NZ * NY)
    width = down_weight.shape[2]
    ranks = down_shrink.shape[2]
    band = NZ * share
    per = ranks // (NZ * NY)
    fence = lax.optimization_barrier
    place = jnp.stack([z, y]).astype(jnp.int32)

    up_own = down_up_factors[0]
    ups = [up_own] + [send(up_own, 0, d) for d in (1, 2, 3)]

    far_a, far_b, low_own, *low_parts = far_products(
        place, hidden, down_weight, down_shrink, share
    )
    in_a, in_b = send(far_a, 0, 1), send(far_b, 0, NY - 1)
    low_in = [send(low_parts[d - 1], 0, d) for d in (1, 2, 3)]
    right, left = rest_products(
        place, after(hidden, (far_a, ups)), down_weight, share, (1, 3)
    )
    my_ids = lax.dynamic_slice_in_dim(tenant_ids.reshape(NZ, NY, share), y, 1, 1).reshape(band)
    my_scale = adapter_scale(my_ids, adapter_rank, adapter_offset, jnp.arange(ranks))
    in_a, in_b, low_in, right, left, my_scale = fence(
        (in_a, in_b, low_in, right, left, my_scale)
    )

    right, left = fold(right, left, in_a, in_b)
    from_left, from_right = send(right, 0, 1), send(left, 0, NY - 1)
    low_y = low_own + sum(part.astype(F32) for part in low_in)
    low_out = low_y.astype(BF)
    low = [low_y] + [send(low_out, e, 0) for e in (2, 1, 3)]
    (own,) = rest_products(place, after(hidden, right), down_weight, share, (0,))
    from_left, from_right, low, my_scale, own, tenant_ids, qkv_expand = fence(
        (from_left, from_right, low, my_scale, own, tenant_ids, qkv_expand)
    )

    pieces = totals(share, place, (own, from_left, from_right), low, my_scale, ups)
    swapped = [send(pieces[e], e, 0) for e in (1, 3, 2)]
    arrived_ids = send(tenant_ids, 0, 0, 1)
    down_own = after(qkv_shrink[0].T, arrived_ids)
    down = [down_own] + [send(down_own, 0, d) for d in (1, 2)]
    swapped, arrived_ids = fence((swapped, arrived_ids))
    block = residual.astype(F32) + pieces[0]
    for part in swapped:
        block = block + part.astype(F32)
    stream = block.astype(BF)

    passed = [send(stream, e, 0, 1) for e in (0, 3, 1, 2)]
    ids = lax.dynamic_slice_in_dim(arrived_ids.reshape(NZ, NY, share), y, 1, 1).reshape(band)
    numbers = z * (NY * per) + jnp.arange(NY * per)
    scale = adapter_scale(ids, adapter_rank, adapter_offset, numbers).T
    expand = qkv_expand[0]
    down.append(send(after(down_own, swapped), 0, 3))
    passed, scale, expand, down = fence((passed, scale, expand, down))
    block, small = normalised(
        share, place, (passed[0], passed[2], passed[3], passed[1]), norm_gain, down, scale
    )

    matrix = qkv_weight[0].T
    from_left, from_right = send(block, 0, 1), send(block, 0, NY - 1)
    small = jnp.concatenate([small] + [send(small, e, 0) for e in (1, 2, 3)], axis=0)
    near = near_products(place, (block,), matrix)
    small = [small] + [send(small, 0, d) for d in (1, 2, 3)]
    from_left, from_right, small, near = fence((from_left, from_right, small, near))
    half = band // 2
    far_a = send(from_left[:half], 0, 1)
    far_b = send(from_right[half:], 0, NY - 1)
    joined = joined_products(share, place, from_right, from_left, matrix, near[0], small, expand)
    far_a, far_b, joined = fence((far_a, far_b, joined))
    out = output_products(share, place, far_a, far_b, matrix, joined)
    return stream, out.T


def solution(mesh):
    in_specs = (
        P("section", "tensor"),
        P("section", "tensor", None),
        P("section", "tensor", None),
        P("section", None, "tensor"),
        P(("section", "tensor"), None),
        P("section"),
        P(),
        P(),
        P("section", None),
        P("section", None, "tensor"),
        P("section", None, "tensor"),
        P("section", None, "tensor"),
    )
    out_specs = (P(("section", "tensor"), None), P("section", "tensor"))
    return jax.shard_map(
        per_device, mesh=mesh, in_specs=in_specs, out_specs=out_specs, check_vma=False
    )
```

```python
import functools

import jax
import jax.numpy as jnp
from jax import lax
from jax.experimental import pallas as pl
from jax.experimental.pallas import tpu as pltpu
from jax.sharding import PartitionSpec as P

adapter_alpha_scale = 32.0
BF = jnp.bfloat16
F32 = jnp.float32
NZ = 4
NY = 4
PIECES = 2
VMEM_BYTES = 40 << 20


def send(block, dz=0, dy=0, ds=0):
    sections = lax.axis_size("section")
    group = NZ * NY
    route = []
    for s in range(sections):
        for z in range(NZ):
            for y in range(NY):
                to = ((s + ds) % sections) * group + ((z + dz) % NZ) * NY + (y + dy) % NY
                route.append((s * group + z * NY + y, to))
    return lax.ppermute(block, ("section", "tensor"), route)


def after(block, done):
    return lax.optimization_barrier((block, done))[0]


def table_lookup(table, tenants):
    chosen = tenants[:, None] == jnp.arange(table.shape[0], dtype=jnp.int32)[None, :]
    return jnp.sum(jnp.where(chosen, table[None, :], 0), axis=1)


def adapter_scale(tenants, adapter_rank, adapter_offset, columns):
    lower = table_lookup(adapter_offset, tenants)
    tenant_ranks = table_lookup(adapter_rank, tenants)
    inside = (columns[None, :] >= lower[:, None]) & (
        columns[None, :] < (lower + tenant_ranks)[:, None]
    )
    scaling_factor = adapter_alpha_scale / tenant_ranks.astype(F32)
    return jnp.where(inside, scaling_factor[:, None], F32(0.0))


def dot(a, b):
    return jnp.dot(a, b, preferred_element_type=F32)


def rows_times(block, matrix):
    return lax.dot_general(
        block, matrix, (((1,), (1,)), ((), ())), preferred_element_type=F32
    )


def staged_call(body, place, inputs, outputs, scratch, flops):
    n_in, n_out = len(inputs), len(outputs)

    def kernel(place, *refs):
        sources, targets = refs[:n_in], refs[n_in : n_in + n_out]
        held, made = refs[n_in + n_out : 2 * n_in + n_out], refs[2 * n_in + n_out : -2]
        in_sem, out_sem = refs[-2:]
        loads = [
            pltpu.make_async_copy(sources[i], held[i], in_sem.at[i]) for i in range(n_in)
        ]
        stores = [
            pltpu.make_async_copy(made[i], targets[i], out_sem.at[i]) for i in range(n_out)
        ]
        for load in loads:
            load.start()

        def ready(i):
            loads[i].wait()
            return held[i]

        def emit(i, value):
            made[i][...] = value
            stores[i].start()

        body(place, ready, emit, made[n_out:])
        for store in stores:
            store.wait()

    hbm = pl.BlockSpec(memory_space=pltpu.MemorySpace.HBM)
    return pl.pallas_call(
        kernel,
        in_specs=[pl.BlockSpec(memory_space=pltpu.MemorySpace.SMEM)] + [hbm] * n_in,
        out_specs=[hbm] * n_out,
        out_shape=outputs,
        scratch_shapes=[pltpu.VMEM(a.shape, a.dtype) for a in list(inputs) + list(outputs)]
        + scratch
        + [pltpu.SemaphoreType.DMA((n_in,)), pltpu.SemaphoreType.DMA((n_out,))],
        compiler_params=pltpu.CompilerParams(vmem_limit_bytes=VMEM_BYTES),
        cost_estimate=pl.CostEstimate(flops=flops, bytes_accessed=8 << 20, transcendentals=0),
    )(place, *inputs)


def pieces_of(weight, hidden, count):
    depth = weight.shape[0]
    cuts = [depth * k // (128 * count) * 128 for k in range(count)] + [depth]
    return list(zip(cuts[:-1], cuts[1:]))


def down_call(kernel, place, hidden, weight, outputs, scratch, more, flops):
    hbm = pl.BlockSpec(memory_space=pltpu.MemorySpace.HBM)
    rows, ff = hidden.shape
    return pl.pallas_call(
        kernel,
        in_specs=[pl.BlockSpec(memory_space=pltpu.MemorySpace.SMEM)] + [hbm] * (2 + len(more)),
        out_specs=[hbm] * len(outputs),
        out_shape=outputs,
        scratch_shapes=[
            pltpu.VMEM((rows, ff), BF),
            pltpu.VMEM((rows, ff), BF),
            pltpu.VMEM((ff, weight.shape[2]), BF),
            pltpu.SemaphoreType.DMA(()),
            pltpu.SemaphoreType.DMA((PIECES,)),
            pltpu.SemaphoreType.DMA((len(outputs),)),
            *[pltpu.VMEM(a.shape, a.dtype) for a in outputs],
            *scratch,
        ],
        compiler_params=pltpu.CompilerParams(vmem_limit_bytes=(58 << 20)),
        cost_estimate=pl.CostEstimate(
            flops=flops, bytes_accessed=2 * (rows * ff + ff * weight.shape[2]), transcendentals=0
        ),
    )(place, hidden, weight, *more)


def weight_loads(weight, taps, sem):
    loads = []
    for k, (low, high) in enumerate(pieces_of(taps, None, PIECES)):
        rows = pl.ds(low, high - low)
        loads.append(
            pltpu.make_async_copy(weight.at[0, rows, :], taps.at[rows, :], sem.at[k])
        )
    return loads


def reordered(place, raw, acts, share, distances):
    for i, d in enumerate(distances):
        y_at = lax.rem(place[1] + d, NY)
        for zz in range(NZ):
            start = pl.multiple_of((zz * NY + y_at) * share, share)
            k = i * NZ + zz
            acts[k * share : (k + 1) * share, :] = raw[pl.ds(start, share), :].astype(acts.dtype)


def far_kernel(
    share, place, hidden, weight, shrink, far_a, far_b, low, low_1, low_2, low_3, raw, acts, taps,
    raw_sem, taps_sem, out_sem, *rest
):
    made, (acc, low_all, shrink_in, shrink_sem) = rest[:6], rest[6:]
    band = NZ * share
    half = taps.shape[1] // 2
    load = pltpu.make_async_copy(hidden, raw, raw_sem)
    small = pltpu.make_async_copy(shrink.at[0], shrink_in, shrink_sem)
    loads = weight_loads(weight, taps, taps_sem)
    stores = [
        pltpu.make_async_copy(made[i], target, out_sem.at[i])
        for i, target in enumerate((far_a, far_b, low, low_1, low_2, low_3))
    ]
    for copy in [load, small, *loads]:
        copy.start()
    load.wait()
    reordered(place, raw, acts, share, (2,))
    small.wait()
    low_all[...] = dot(raw[...], shrink_in[...])
    for d in range(NY):
        reordered(place, low_all, made[2 + d], share, (d,))
        stores[2 + d].start()
    cuts = pieces_of(taps, None, PIECES)
    for k, (first, last) in enumerate(cuts):
        loads[k].wait()
        part = dot(acts[:band, first:last], taps[first:last, :])
        if k > 0:
            part = acc[...] + part
        if k < len(cuts) - 1:
            acc[...] = part
        else:
            made[0][...] = part[:, :half].astype(BF)
            stores[0].start()
            made[1][...] = part[:, half:].astype(BF)
            stores[1].start()
    for store in stores:
        store.wait()


def far_products(place, hidden, weight, shrink, share):
    rows, ff = hidden.shape
    width, ranks = weight.shape[2], shrink.shape[2]
    band = NZ * share
    outputs = [jax.ShapeDtypeStruct((band, width // 2), BF)] * 2
    outputs += [jax.ShapeDtypeStruct((band, ranks), F32)]
    outputs += [jax.ShapeDtypeStruct((band, ranks), BF)] * 3
    scratch = [
        pltpu.VMEM((band, width), F32),
        pltpu.VMEM((rows, ranks), F32),
        pltpu.VMEM((ff, ranks), BF),
        pltpu.SemaphoreType.DMA(()),
    ]
    return down_call(
        functools.partial(far_kernel, share), place, hidden, weight, outputs, scratch, [shrink],
        2 * ff * (band * width + rows * ranks),
    )


def rest_kernel(share, distances, place, hidden, weight, *refs):
    count = len(distances)
    targets, refs = refs[:count], refs[count:]
    raw, acts, taps, raw_sem, taps_sem, out_sem, *made = refs
    made, acc = made[:count], made[count]
    band = NZ * share
    load = pltpu.make_async_copy(hidden, raw, raw_sem)
    loads = weight_loads(weight, taps, taps_sem)
    stores = [pltpu.make_async_copy(made[i], targets[i], out_sem.at[i]) for i in range(count)]
    for copy in [load, *loads]:
        copy.start()
    load.wait()
    reordered(place, raw, acts, share, distances)
    cuts = pieces_of(taps, None, PIECES)
    for k, (first, last) in enumerate(cuts):
        loads[k].wait()
        for i in range(count):
            rows = slice(i * band, (i + 1) * band)
            part = dot(acts[rows, first:last], taps[first:last, :])
            if k > 0:
                part = acc[rows, :] + part
            if k < len(cuts) - 1:
                acc[rows, :] = part
            else:
                made[i][...] = part.astype(BF)
                stores[i].start()
    for store in stores:
        store.wait()


def rest_products(place, hidden, weight, share, distances):
    rows, ff = hidden.shape
    width = weight.shape[2]
    band = NZ * share
    count = len(distances)
    return down_call(
        functools.partial(rest_kernel, share, distances), place, hidden, weight,
        [jax.ShapeDtypeStruct((band, width), BF)] * count,
        [pltpu.VMEM((count * band, width), F32)], [], 2 * count * band * ff * width,
    )


def fold_kernel(right, left, in_a, in_b, right_out, left_out, base, more, sem, out_sem):
    half = in_a.shape[1]
    sides = ((right, in_a, right_out, 0), (left, in_b, left_out, half))
    loads, stores = [], []
    for i, (whole, arrived, target, first) in enumerate(sides):
        columns = pl.ds(first, half)
        loads.append(pltpu.make_async_copy(whole.at[:, columns], base.at[i], sem.at[2 * i]))
        loads.append(pltpu.make_async_copy(arrived, more.at[i], sem.at[2 * i + 1]))
        stores.append(pltpu.make_async_copy(base.at[i], target.at[:, columns], out_sem.at[i]))
    for load in loads:
        load.start()
    for i in range(2):
        loads[2 * i].wait()
        loads[2 * i + 1].wait()
        base[i] = (base[i].astype(F32) + more[i].astype(F32)).astype(BF)
        stores[i].start()
    for store in stores:
        store.wait()


def fold(right, left, in_a, in_b):
    hbm = pl.BlockSpec(memory_space=pltpu.MemorySpace.HBM)
    return pl.pallas_call(
        fold_kernel,
        in_specs=[hbm] * 4,
        out_specs=[hbm] * 2,
        out_shape=[jax.ShapeDtypeStruct(right.shape, BF)] * 2,
        input_output_aliases={0: 0, 1: 1},
        scratch_shapes=[
            pltpu.VMEM((2, *in_a.shape), BF),
            pltpu.VMEM((2, *in_a.shape), BF),
            pltpu.SemaphoreType.DMA((4,)),
            pltpu.SemaphoreType.DMA((2,)),
        ],
        compiler_params=pltpu.CompilerParams(vmem_limit_bytes=VMEM_BYTES),
        cost_estimate=pl.CostEstimate(
            flops=right.size, bytes_accessed=6 * right.size, transcendentals=0
        ),
    )(right, left, in_a, in_b)


def total_kernel(
    share, place, low, low_1, low_2, low_3, scale, up_0, up_1, up_2, up_3, own, left, right,
    out_0, out_1, out_2, out_3, low_in, more_in, scale_in, up_in, parts, added, total, piece_0,
    pieces, low_sem, part_sem, out_sem
):
    tile = up_0.shape[1]
    wide = NY * tile
    order = (2, 1, 3, 0)
    outs = (out_0, out_1, out_2, out_3)

    def rows_of(e):
        return pl.ds(pl.multiple_of(lax.rem(place[0] + e, NZ) * share, share), share)

    loads = [
        pltpu.make_async_copy(low, low_in, low_sem.at[0]),
        pltpu.make_async_copy(scale, scale_in, low_sem.at[1]),
    ]
    for i, source in enumerate((low_1, low_2, low_3)):
        loads.append(pltpu.make_async_copy(source, more_in.at[i], low_sem.at[2 + i]))
    for i, source in enumerate((up_0, up_1, up_2, up_3)):
        loads.append(
            pltpu.make_async_copy(
                source.at[pl.ds(0, low.shape[1]), :], up_in.at[i], low_sem.at[5 + i]
            )
        )
    part_loads = {
        e: [
            pltpu.make_async_copy(
                source.at[rows_of(e), :], parts.at[i, pl.ds(e * share, share), :], part_sem.at[e, i]
            )
            for i, source in enumerate((own, left, right))
        ]
        for e in order
    }
    stores = [
        pltpu.make_async_copy(
            piece_0 if e == 0 else pieces.at[e - 1], outs[e], out_sem.at[e]
        )
        for e in range(NZ)
    ]
    for load in loads:
        load.start()
    for e in order:
        for load in part_loads[e]:
            load.start()
    for load in loads:
        load.wait()
    low_sum = low_in[...]
    for i in range(3):
        low_sum = low_sum + more_in[i].astype(F32)
    rows = (low_sum * scale_in[...]).astype(BF)
    for d in range(NY):
        at = lax.rem(place[1] + NY - d, NY) * tile
        added[:, pl.ds(pl.multiple_of(at, tile), tile)] = dot(rows, up_in[d])
    columns = pl.ds(pl.multiple_of(place[0] * wide, wide), wide)
    for e in order:
        for load in part_loads[e]:
            load.wait()
        at = slice(e * share, (e + 1) * share)
        total[...] = (
            parts[0, at, :].astype(F32) + parts[1, at, :].astype(F32) + parts[2, at, :].astype(F32)
        )
        total[:, columns] += added[rows_of(e), :]
        if e == 0:
            piece_0[...] = total[...]
        else:
            pieces[e - 1] = total[...].astype(BF)
        stores[e].start()
    for store in stores:
        store.wait()


def totals(share, place, parts, low, scale, ups):
    band, width = parts[0].shape
    ranks, tile = low[0].shape[1], ups[0].shape[1]
    hbm = pl.BlockSpec(memory_space=pltpu.MemorySpace.HBM)
    return pl.pallas_call(
        functools.partial(total_kernel, share),
        in_specs=[pl.BlockSpec(memory_space=pltpu.MemorySpace.SMEM)] + [hbm] * 12,
        out_specs=[hbm] * 4,
        out_shape=[jax.ShapeDtypeStruct((share, width), F32)]
        + [jax.ShapeDtypeStruct((share, width), BF)] * 3,
        scratch_shapes=[
            pltpu.VMEM((band, ranks), F32),
            pltpu.VMEM((3, band, ranks), BF),
            pltpu.VMEM((band, ranks), F32),
            pltpu.VMEM((NY, ranks, tile), BF),
            pltpu.VMEM((3, band, width), BF),
            pltpu.VMEM((band, NY * tile), F32),
            pltpu.VMEM((share, width), F32),
            pltpu.VMEM((share, width), F32),
            pltpu.VMEM((3, share, width), BF),
            pltpu.SemaphoreType.DMA((9,)),
            pltpu.SemaphoreType.DMA((NZ, 3)),
            pltpu.SemaphoreType.DMA((NZ,)),
        ],
        compiler_params=pltpu.CompilerParams(vmem_limit_bytes=58 << 20),
        cost_estimate=pl.CostEstimate(
            flops=2 * band * width * 128, bytes_accessed=10 * band * width, transcendentals=0
        ),
    )(place, *low, scale, *ups, *parts)


def normalised(share, place, pieces, gain, factors, scale):
    width = pieces[0].shape[1]
    per = factors[0].shape[0]
    band = NZ * share

    def body(place, ready, emit, scratch):
        block, taps = scratch
        gain = ready(0)[...].astype(F32)
        for e in range(NZ):
            values = ready(1 + e)[...].astype(F32)
            mean = jnp.mean(values * values, axis=1, keepdims=True)
            at = pl.multiple_of(lax.rem(place[0] + NZ - e, NZ) * share, share)
            block[pl.ds(at, share), :] = (values * lax.rsqrt(mean + 1e-05) * gain).astype(BF)
        emit(0, block[...])
        for d in range(NY):
            at = pl.multiple_of(lax.rem(place[1] + NY - d, NY) * per, per)
            taps[pl.ds(at, per), :] = ready(1 + NZ + d)[...]
        emit(1, (rows_times(taps[...], block[...]) * ready(1 + NZ + NY)[...]).astype(BF))

    outputs = [
        jax.ShapeDtypeStruct((band, width), BF),
        jax.ShapeDtypeStruct((NY * per, band), BF),
    ]
    scratch = [pltpu.VMEM((band, width), BF), pltpu.VMEM((NY * per, width), BF)]
    return staged_call(
        body, place, (gain, *pieces, *factors, scale), outputs, scratch, 2 * band * width * 128
    )


def near_products(place, blocks, matrix):
    rows, cols = blocks[0].shape[0], matrix.shape[0]
    count = len(blocks)

    def body(place, ready, emit, scratch):
        taps = ready(0)
        for i in range(count):
            emit(i, rows_times(ready(1 + i)[...], taps[...]))

    outputs = [jax.ShapeDtypeStruct((rows, cols), F32)] * count
    flops = 2 * count * rows * cols * matrix.shape[1]
    return staged_call(body, place, (matrix, *blocks), outputs, [], flops)


def joined_products(share, place, right, left, matrix, own, small, expand):
    cols, ranks = matrix.shape[0], expand.shape[0]
    band = NZ * share
    wide = ranks // NZ

    def body(place, ready, emit, scratch):
        acc, factors = scratch
        held = ready(0)
        for e in range(NZ):
            at = pl.multiple_of(lax.rem(place[0] + NZ - e, NZ) * wide, wide)
            factors[e * wide : (e + 1) * wide, :] = held[pl.ds(at, wide), :]

        def put(d, part):
            put_rows(share, place, acc, d, part)

        def adapter(i):
            return lax.dot_general(
                ready(1 + i)[...], factors[...], (((0,), (0,)), ((), ())),
                preferred_element_type=F32,
            )

        put(2, adapter(2))
        put(0, ready(5)[...] + adapter(0))
        taps = ready(6)
        put(1, adapter(3) + rows_times(ready(7)[...], taps[...]))
        put(3, adapter(1) + rows_times(ready(8)[...], taps[...]))
        emit(0, acc[...])

    return staged_call(
        body,
        place,
        (expand, *small, own, matrix, right, left),
        [jax.ShapeDtypeStruct((NY * band, cols), F32)],
        [pltpu.VMEM((NY * band, cols), F32), pltpu.VMEM((ranks, cols), BF)],
        4 * band * cols * matrix.shape[1],
    )[0]


def put_rows(share, place, acc, d, part, add=False):
    y_at = lax.rem(place[1] + d, NY)
    for zz in range(NZ):
        at = pl.ds(pl.multiple_of((zz * NY + y_at) * share, share), share)
        rows = part[zz * share : (zz + 1) * share]
        acc[at, :] = acc[at, :] + rows if add else rows


def output_products(share, place, far_a, far_b, matrix, joined):
    rows, cols = joined.shape

    def body(place, ready, emit, scratch):
        taps = ready(0)
        part = jnp.concatenate(
            [rows_times(ready(1)[...], taps[...]), rows_times(ready(2)[...], taps[...])], axis=0
        )
        acc = ready(3)
        put_rows(share, place, acc, 2, part, True)
        emit(0, acc[...].T.astype(BF))

    return staged_call(
        body, place, (matrix, far_a, far_b, joined),
        [jax.ShapeDtypeStruct((cols, rows), BF)], [], 4 * far_a.size * cols,
    )[0]


def per_device(
    hidden,
    down_weight,
    down_shrink,
    down_up_factors,
    residual,
    tenant_ids,
    adapter_rank,
    adapter_offset,
    norm_gain,
    qkv_weight,
    qkv_shrink,
    qkv_expand,
):
    my_index = lax.axis_index("tensor")
    z, y = my_index // NY, my_index % NY
    rows, ff = hidden.shape
    share = rows // (NZ * NY)
    width = down_weight.shape[2]
    ranks = down_shrink.shape[2]
    band = NZ * share
    per = ranks // (NZ * NY)
    fence = lax.optimization_barrier
    place = jnp.stack([z, y]).astype(jnp.int32)

    up_own = down_up_factors[0]
    ups = [up_own] + [send(up_own, 0, d) for d in (1, 2, 3)]

    far_a, far_b, low_own, *low_parts = far_products(
        place, hidden, down_weight, down_shrink, share
    )
    in_a, in_b = send(far_a, 0, 1), send(far_b, 0, NY - 1)
    low_in = [send(low_parts[d - 1], 0, d) for d in (1, 2, 3)]
    right, left = rest_products(
        place, after(hidden, (far_a, ups)), down_weight, share, (1, 3)
    )
    my_ids = lax.dynamic_slice_in_dim(tenant_ids.reshape(NZ, NY, share), y, 1, 1).reshape(band)
    my_scale = adapter_scale(my_ids, adapter_rank, adapter_offset, jnp.arange(ranks))
    in_a, in_b, low_in, right, left, my_scale = fence(
        (in_a, in_b, low_in, right, left, my_scale)
    )

    right, left = fold(right, left, in_a, in_b)
    from_left, from_right = send(right, 0, 1), send(left, 0, NY - 1)
    low_y = low_own + sum(part.astype(F32) for part in low_in)
    low_out = low_y.astype(BF)
    low = [low_y] + [send(low_out, e, 0) for e in (2, 1, 3)]
    (own,) = rest_products(place, after(hidden, right), down_weight, share, (0,))
    from_left, from_right, low, my_scale, own, tenant_ids, qkv_expand = fence(
        (from_left, from_right, low, my_scale, own, tenant_ids, qkv_expand)
    )

    pieces = totals(share, place, (own, from_left, from_right), low, my_scale, ups)
    swapped = [send(pieces[e], e, 0) for e in (1, 3, 2)]
    arrived_ids = send(tenant_ids, 0, 0, 1)
    down_own = after(qkv_shrink[0].T, arrived_ids)
    down = [down_own] + [send(down_own, 0, d) for d in (1, 2)]
    swapped, arrived_ids = fence((swapped, arrived_ids))
    block = residual.astype(F32) + pieces[0]
    for part in swapped:
        block = block + part.astype(F32)
    stream = block.astype(BF)

    passed = [send(stream, e, 0, 1) for e in (0, 3, 1, 2)]
    ids = lax.dynamic_slice_in_dim(arrived_ids.reshape(NZ, NY, share), y, 1, 1).reshape(band)
    numbers = z * (NY * per) + jnp.arange(NY * per)
    scale = adapter_scale(ids, adapter_rank, adapter_offset, numbers).T
    expand = qkv_expand[0]
    down.append(send(after(down_own, swapped), 0, 3))
    passed, scale, expand, down = fence((passed, scale, expand, down))
    block, small = normalised(
        share, place, (passed[0], passed[2], passed[3], passed[1]), norm_gain, down, scale
    )

    matrix = qkv_weight[0].T
    from_left, from_right = send(block, 0, 1), send(block, 0, NY - 1)
    small = jnp.concatenate([small] + [send(small, e, 0) for e in (1, 2, 3)], axis=0)
    near = near_products(place, (block,), matrix)
    small = [small] + [send(small, 0, d) for d in (1, 2, 3)]
    from_left, from_right, small, near = fence((from_left, from_right, small, near))
    half = band // 2
    far_a = send(from_left[:half], 0, 1)
    far_b = send(from_right[half:], 0, NY - 1)
    joined = joined_products(share, place, from_right, from_left, matrix, near[0], small, expand)
    far_a, far_b, joined = fence((far_a, far_b, joined))
    out = output_products(share, place, far_a, far_b, matrix, joined)
    return stream, out.T


def solution(mesh):
    in_specs = (
        P("section", "tensor"),
        P("section", "tensor", None),
        P("section", "tensor", None),
        P("section", None, "tensor"),
        P(("section", "tensor"), None),
        P("section"),
        P(),
        P(),
        P("section", None),
        P("section", None, "tensor"),
        P("section", None, "tensor"),
        P("section", None, "tensor"),
    )
    out_specs = (P(("section", "tensor"), None), P("section", "tensor"))
    return jax.shard_map(
        per_device, mesh=mesh, in_specs=in_specs, out_specs=out_specs, check_vma=False
    )
```

```python
import functools

import jax
import jax.numpy as jnp
from jax import lax
from jax.experimental import pallas as pl
from jax.experimental.pallas import tpu as pltpu
from jax.sharding import PartitionSpec as P

adapter_alpha_scale = 32.0
BF = jnp.bfloat16
F32 = jnp.float32
NZ = 4
NY = 4
PIECES = 2
VMEM_BYTES = 40 << 20


def send(block, dz=0, dy=0, ds=0):
    sections = lax.axis_size("section")
    group = NZ * NY
    route = []
    for s in range(sections):
        for z in range(NZ):
            for y in range(NY):
                to = ((s + ds) % sections) * group + ((z + dz) % NZ) * NY + (y + dy) % NY
                route.append((s * group + z * NY + y, to))
    return lax.ppermute(block, ("section", "tensor"), route)


def swap(block, y_bit):
    sections = lax.axis_size("section")
    places = range(sections * NZ * NY)
    return lax.ppermute(block, ("section", "tensor"), [(i, i ^ y_bit) for i in places])


def after(block, done):
    return lax.optimization_barrier((block, done))[0]


def table_lookup(table, tenants):
    chosen = tenants[:, None] == jnp.arange(table.shape[0], dtype=jnp.int32)[None, :]
    return jnp.sum(jnp.where(chosen, table[None, :], 0), axis=1)


def adapter_scale(tenants, adapter_rank, adapter_offset, columns):
    lower = table_lookup(adapter_offset, tenants)
    tenant_ranks = table_lookup(adapter_rank, tenants)
    inside = (columns[None, :] >= lower[:, None]) & (
        columns[None, :] < (lower + tenant_ranks)[:, None]
    )
    scaling_factor = adapter_alpha_scale / tenant_ranks.astype(F32)
    return jnp.where(inside, scaling_factor[:, None], F32(0.0))


def dot(a, b):
    return jnp.dot(a, b, preferred_element_type=F32)


def rows_times(block, matrix):
    return lax.dot_general(
        block, matrix, (((1,), (1,)), ((), ())), preferred_element_type=F32
    )


def staged_call(body, place, inputs, outputs, scratch, flops):
    n_in, n_out = len(inputs), len(outputs)

    def kernel(place, *refs):
        sources, targets = refs[:n_in], refs[n_in : n_in + n_out]
        held, made = refs[n_in + n_out : 2 * n_in + n_out], refs[2 * n_in + n_out : -2]
        in_sem, out_sem = refs[-2:]
        loads = [
            pltpu.make_async_copy(sources[i], held[i], in_sem.at[i]) for i in range(n_in)
        ]
        stores = [
            pltpu.make_async_copy(made[i], targets[i], out_sem.at[i]) for i in range(n_out)
        ]
        for load in loads:
            load.start()

        def ready(i):
            loads[i].wait()
            return held[i]

        def emit(i, value):
            made[i][...] = value
            stores[i].start()

        body(place, ready, emit, made[n_out:])
        for store in stores:
            store.wait()

    hbm = pl.BlockSpec(memory_space=pltpu.MemorySpace.HBM)
    return pl.pallas_call(
        kernel,
        in_specs=[pl.BlockSpec(memory_space=pltpu.MemorySpace.SMEM)] + [hbm] * n_in,
        out_specs=[hbm] * n_out,
        out_shape=outputs,
        scratch_shapes=[pltpu.VMEM(a.shape, a.dtype) for a in list(inputs) + list(outputs)]
        + scratch
        + [pltpu.SemaphoreType.DMA((n_in,)), pltpu.SemaphoreType.DMA((n_out,))],
        compiler_params=pltpu.CompilerParams(vmem_limit_bytes=VMEM_BYTES),
        cost_estimate=pl.CostEstimate(flops=flops, bytes_accessed=8 << 20, transcendentals=0),
    )(place, *inputs)


def pieces_of(weight, hidden, count):
    depth = weight.shape[0]
    cuts = [depth * k // (128 * count) * 128 for k in range(count)] + [depth]
    return list(zip(cuts[:-1], cuts[1:]))


def down_call(kernel, place, hidden, weight, outputs, scratch, more, flops):
    hbm = pl.BlockSpec(memory_space=pltpu.MemorySpace.HBM)
    rows, ff = hidden.shape
    return pl.pallas_call(
        kernel,
        in_specs=[pl.BlockSpec(memory_space=pltpu.MemorySpace.SMEM)] + [hbm] * (2 + len(more)),
        out_specs=[hbm] * len(outputs),
        out_shape=outputs,
        scratch_shapes=[
            pltpu.VMEM((rows, ff), BF),
            pltpu.VMEM((rows, ff), BF),
            pltpu.VMEM((ff, weight.shape[2]), BF),
            pltpu.SemaphoreType.DMA(()),
            pltpu.SemaphoreType.DMA((PIECES,)),
            pltpu.SemaphoreType.DMA((len(outputs),)),
            *[pltpu.VMEM(a.shape, a.dtype) for a in outputs],
            *scratch,
        ],
        compiler_params=pltpu.CompilerParams(vmem_limit_bytes=(58 << 20)),
        cost_estimate=pl.CostEstimate(
            flops=flops, bytes_accessed=2 * (rows * ff + ff * weight.shape[2]), transcendentals=0
        ),
    )(place, hidden, weight, *more)


def weight_loads(weight, taps, sem):
    loads = []
    for k, (low, high) in enumerate(pieces_of(taps, None, PIECES)):
        rows = pl.ds(low, high - low)
        loads.append(
            pltpu.make_async_copy(weight.at[0, rows, :], taps.at[rows, :], sem.at[k])
        )
    return loads


def reordered(place, raw, acts, share, distances):
    for i, d in enumerate(distances):
        y_at = lax.rem(place[1] + d, NY)
        for zz in range(NZ):
            start = pl.multiple_of((zz * NY + y_at) * share, share)
            k = i * NZ + zz
            acts[k * share : (k + 1) * share, :] = raw[pl.ds(start, share), :].astype(acts.dtype)


def far_kernel(
    share, place, hidden, weight, shrink, far_a, far_b, low, low_1, low_2, low_3, raw, acts, taps,
    raw_sem, taps_sem, out_sem, *rest
):
    made, (acc, low_all, shrink_in, shrink_sem) = rest[:6], rest[6:]
    band = NZ * share
    half = taps.shape[1] // 2
    load = pltpu.make_async_copy(hidden, raw, raw_sem)
    small = pltpu.make_async_copy(shrink.at[0], shrink_in, shrink_sem)
    loads = weight_loads(weight, taps, taps_sem)
    stores = [
        pltpu.make_async_copy(made[i], target, out_sem.at[i])
        for i, target in enumerate((far_a, far_b, low, low_1, low_2, low_3))
    ]
    for copy in [load, small, *loads]:
        copy.start()
    load.wait()
    reordered(place, raw, acts, share, (2,))
    small.wait()
    low_all[...] = dot(raw[...], shrink_in[...])
    for d in range(NY):
        reordered(place, low_all, made[2 + d], share, (d,))
        stores[2 + d].start()
    cuts = pieces_of(taps, None, PIECES)
    for k, (first, last) in enumerate(cuts):
        loads[k].wait()
        part = dot(acts[:band, first:last], taps[first:last, :])
        if k > 0:
            part = acc[...] + part
        if k < len(cuts) - 1:
            acc[...] = part
        else:
            made[0][...] = part[:, :half].astype(BF)
            stores[0].start()
            made[1][...] = part[:, half:].astype(BF)
            stores[1].start()
    for store in stores:
        store.wait()


def far_products(place, hidden, weight, shrink, share):
    rows, ff = hidden.shape
    width, ranks = weight.shape[2], shrink.shape[2]
    band = NZ * share
    outputs = [jax.ShapeDtypeStruct((band, width // 2), BF)] * 2
    outputs += [jax.ShapeDtypeStruct((band, ranks), F32)]
    outputs += [jax.ShapeDtypeStruct((band, ranks), BF)] * 3
    scratch = [
        pltpu.VMEM((band, width), F32),
        pltpu.VMEM((rows, ranks), F32),
        pltpu.VMEM((ff, ranks), BF),
        pltpu.SemaphoreType.DMA(()),
    ]
    return down_call(
        functools.partial(far_kernel, share), place, hidden, weight, outputs, scratch, [shrink],
        2 * ff * (band * width + rows * ranks),
    )


def rest_kernel(share, distances, place, hidden, weight, *refs):
    count = len(distances)
    targets, refs = refs[:count], refs[count:]
    raw, acts, taps, raw_sem, taps_sem, out_sem, *made = refs
    made, acc = made[:count], made[count]
    band = NZ * share
    load = pltpu.make_async_copy(hidden, raw, raw_sem)
    loads = weight_loads(weight, taps, taps_sem)
    stores = [pltpu.make_async_copy(made[i], targets[i], out_sem.at[i]) for i in range(count)]
    for copy in [load, *loads]:
        copy.start()
    load.wait()
    reordered(place, raw, acts, share, distances)
    cuts = pieces_of(taps, None, PIECES)
    for k, (first, last) in enumerate(cuts):
        loads[k].wait()
        for i in range(count):
            rows = slice(i * band, (i + 1) * band)
            part = dot(acts[rows, first:last], taps[first:last, :])
            if k > 0:
                part = acc[rows, :] + part
            if k < len(cuts) - 1:
                acc[rows, :] = part
            else:
                made[i][...] = part.astype(BF)
                stores[i].start()
    for store in stores:
        store.wait()


def rest_products(place, hidden, weight, share, distances):
    rows, ff = hidden.shape
    width = weight.shape[2]
    band = NZ * share
    count = len(distances)
    return down_call(
        functools.partial(rest_kernel, share, distances), place, hidden, weight,
        [jax.ShapeDtypeStruct((band, width), BF)] * count,
        [pltpu.VMEM((count * band, width), F32)], [], 2 * count * band * ff * width,
    )


def fold_kernel(right, left, in_a, in_b, right_out, left_out, base, more, sem, out_sem):
    half = in_a.shape[1]
    sides = ((right, in_a, right_out, 0), (left, in_b, left_out, half))
    loads, stores = [], []
    for i, (whole, arrived, target, first) in enumerate(sides):
        columns = pl.ds(first, half)
        loads.append(pltpu.make_async_copy(whole.at[:, columns], base.at[i], sem.at[2 * i]))
        loads.append(pltpu.make_async_copy(arrived, more.at[i], sem.at[2 * i + 1]))
        stores.append(pltpu.make_async_copy(base.at[i], target.at[:, columns], out_sem.at[i]))
    for load in loads:
        load.start()
    for i in range(2):
        loads[2 * i].wait()
        loads[2 * i + 1].wait()
        base[i] = (base[i].astype(F32) + more[i].astype(F32)).astype(BF)
        stores[i].start()
    for store in stores:
        store.wait()


def fold(right, left, in_a, in_b):
    hbm = pl.BlockSpec(memory_space=pltpu.MemorySpace.HBM)
    return pl.pallas_call(
        fold_kernel,
        in_specs=[hbm] * 4,
        out_specs=[hbm] * 2,
        out_shape=[jax.ShapeDtypeStruct(right.shape, BF)] * 2,
        input_output_aliases={0: 0, 1: 1},
        scratch_shapes=[
            pltpu.VMEM((2, *in_a.shape), BF),
            pltpu.VMEM((2, *in_a.shape), BF),
            pltpu.SemaphoreType.DMA((4,)),
            pltpu.SemaphoreType.DMA((2,)),
        ],
        compiler_params=pltpu.CompilerParams(vmem_limit_bytes=VMEM_BYTES),
        cost_estimate=pl.CostEstimate(
            flops=right.size, bytes_accessed=6 * right.size, transcendentals=0
        ),
    )(right, left, in_a, in_b)


def total_kernel(
    share, place, low, low_1, low_2, low_3, scale, up_0, up_1, up_2, up_3, own, left, right,
    out_0, out_1, out_2, out_3, low_in, more_in, scale_in, up_in, parts, added, total, piece_0,
    pieces, low_sem, part_sem, out_sem
):
    tile = up_0.shape[1]
    wide = NY * tile
    order = (2, 1, 3, 0)
    outs = (out_0, out_1, out_2, out_3)

    def rows_of(e):
        return pl.ds(pl.multiple_of(lax.rem(place[0] + e, NZ) * share, share), share)

    loads = [
        pltpu.make_async_copy(low, low_in, low_sem.at[0]),
        pltpu.make_async_copy(scale, scale_in, low_sem.at[1]),
    ]
    for i, source in enumerate((low_1, low_2, low_3)):
        loads.append(pltpu.make_async_copy(source, more_in.at[i], low_sem.at[2 + i]))
    for i, source in enumerate((up_0, up_1, up_2, up_3)):
        loads.append(
            pltpu.make_async_copy(
                source.at[pl.ds(0, low.shape[1]), :], up_in.at[i], low_sem.at[5 + i]
            )
        )
    part_loads = {
        e: [
            pltpu.make_async_copy(
                source.at[rows_of(e), :], parts.at[i, pl.ds(e * share, share), :], part_sem.at[e, i]
            )
            for i, source in enumerate((own, left, right))
        ]
        for e in order
    }
    stores = [
        pltpu.make_async_copy(
            piece_0 if e == 0 else pieces.at[e - 1], outs[e], out_sem.at[e]
        )
        for e in range(NZ)
    ]
    for load in loads:
        load.start()
    for e in order:
        for load in part_loads[e]:
            load.start()
    for load in loads:
        load.wait()
    low_sum = low_in[...]
    for i in range(3):
        low_sum = low_sum + more_in[i].astype(F32)
    rows = (low_sum * scale_in[...]).astype(BF)
    for d in range(NY):
        at = jnp.bitwise_xor(place[1], d) * tile
        added[:, pl.ds(pl.multiple_of(at, tile), tile)] = dot(rows, up_in[d])
    columns = pl.ds(pl.multiple_of(place[0] * wide, wide), wide)
    for e in order:
        for load in part_loads[e]:
            load.wait()
        at = slice(e * share, (e + 1) * share)
        total[...] = (
            parts[0, at, :].astype(F32) + parts[1, at, :].astype(F32) + parts[2, at, :].astype(F32)
        )
        total[:, columns] += added[rows_of(e), :]
        if e == 0:
            piece_0[...] = total[...]
        else:
            pieces[e - 1] = total[...].astype(BF)
        stores[e].start()
    for store in stores:
        store.wait()


def totals(share, place, parts, low, scale, ups):
    band, width = parts[0].shape
    ranks, tile = low[0].shape[1], ups[0].shape[1]
    hbm = pl.BlockSpec(memory_space=pltpu.MemorySpace.HBM)
    return pl.pallas_call(
        functools.partial(total_kernel, share),
        in_specs=[pl.BlockSpec(memory_space=pltpu.MemorySpace.SMEM)] + [hbm] * 12,
        out_specs=[hbm] * 4,
        out_shape=[jax.ShapeDtypeStruct((share, width), F32)]
        + [jax.ShapeDtypeStruct((share, width), BF)] * 3,
        scratch_shapes=[
            pltpu.VMEM((band, ranks), F32),
            pltpu.VMEM((3, band, ranks), BF),
            pltpu.VMEM((band, ranks), F32),
            pltpu.VMEM((NY, ranks, tile), BF),
            pltpu.VMEM((3, band, width), BF),
            pltpu.VMEM((band, NY * tile), F32),
            pltpu.VMEM((share, width), F32),
            pltpu.VMEM((share, width), F32),
            pltpu.VMEM((3, share, width), BF),
            pltpu.SemaphoreType.DMA((9,)),
            pltpu.SemaphoreType.DMA((NZ, 3)),
            pltpu.SemaphoreType.DMA((NZ,)),
        ],
        compiler_params=pltpu.CompilerParams(vmem_limit_bytes=58 << 20),
        cost_estimate=pl.CostEstimate(
            flops=2 * band * width * 128, bytes_accessed=10 * band * width, transcendentals=0
        ),
    )(place, *low, scale, *ups, *parts)


def normalised(share, place, pieces, gain, factors, scale):
    width = pieces[0].shape[1]
    per = factors[0].shape[0]
    band = NZ * share

    def body(place, ready, emit, scratch):
        block, taps = scratch
        gain = ready(0)[...].astype(F32)
        for e in range(NZ):
            values = ready(1 + e)[...].astype(F32)
            mean = jnp.mean(values * values, axis=1, keepdims=True)
            at = pl.multiple_of(lax.rem(place[0] + NZ - e, NZ) * share, share)
            block[pl.ds(at, share), :] = (values * lax.rsqrt(mean + 1e-05) * gain).astype(BF)
        emit(0, block[...])
        for d in range(NY):
            at = pl.multiple_of(lax.rem(place[1] + NY - d, NY) * per, per)
            taps[pl.ds(at, per), :] = ready(1 + NZ + d)[...]
        emit(1, (rows_times(taps[...], block[...]) * ready(1 + NZ + NY)[...]).astype(BF))

    outputs = [
        jax.ShapeDtypeStruct((band, width), BF),
        jax.ShapeDtypeStruct((NY * per, band), BF),
    ]
    scratch = [pltpu.VMEM((band, width), BF), pltpu.VMEM((NY * per, width), BF)]
    return staged_call(
        body, place, (gain, *pieces, *factors, scale), outputs, scratch, 2 * band * width * 128
    )


def near_products(place, blocks, matrix):
    rows, cols = blocks[0].shape[0], matrix.shape[0]
    count = len(blocks)

    def body(place, ready, emit, scratch):
        taps = ready(0)
        for i in range(count):
            emit(i, rows_times(ready(1 + i)[...], taps[...]))

    outputs = [jax.ShapeDtypeStruct((rows, cols), F32)] * count
    flops = 2 * count * rows * cols * matrix.shape[1]
    return staged_call(body, place, (matrix, *blocks), outputs, [], flops)


def joined_products(share, place, right, left, matrix, own, small, expand):
    cols, ranks = matrix.shape[0], expand.shape[0]
    band = NZ * share
    wide = ranks // NZ

    def body(place, ready, emit, scratch):
        acc, factors = scratch
        held = ready(0)
        for e in range(NZ):
            at = pl.multiple_of(lax.rem(place[0] + NZ - e, NZ) * wide, wide)
            factors[e * wide : (e + 1) * wide, :] = held[pl.ds(at, wide), :]

        def put(d, part):
            put_rows(share, place, acc, d, part)

        def adapter(i):
            return lax.dot_general(
                ready(1 + i)[...], factors[...], (((0,), (0,)), ((), ())),
                preferred_element_type=F32,
            )

        put(2, adapter(2))
        put(0, ready(5)[...] + adapter(0))
        taps = ready(6)
        put(1, adapter(3) + rows_times(ready(7)[...], taps[...]))
        put(3, adapter(1) + rows_times(ready(8)[...], taps[...]))
        emit(0, acc[...])

    return staged_call(
        body,
        place,
        (expand, *small, own, matrix, right, left),
        [jax.ShapeDtypeStruct((NY * band, cols), F32)],
        [pltpu.VMEM((NY * band, cols), F32), pltpu.VMEM((ranks, cols), BF)],
        4 * band * cols * matrix.shape[1],
    )[0]


def put_rows(share, place, acc, d, part, add=False):
    y_at = lax.rem(place[1] + d, NY)
    for zz in range(NZ):
        at = pl.ds(pl.multiple_of((zz * NY + y_at) * share, share), share)
        rows = part[zz * share : (zz + 1) * share]
        acc[at, :] = acc[at, :] + rows if add else rows


def output_products(share, place, far_a, far_b, matrix, joined):
    rows, cols = joined.shape

    def body(place, ready, emit, scratch):
        taps = ready(0)
        part = jnp.concatenate(
            [rows_times(ready(1)[...], taps[...]), rows_times(ready(2)[...], taps[...])], axis=0
        )
        acc = ready(3)
        put_rows(share, place, acc, 2, part, True)
        emit(0, acc[...].T.astype(BF))

    return staged_call(
        body, place, (matrix, far_a, far_b, joined),
        [jax.ShapeDtypeStruct((cols, rows), BF)], [], 4 * far_a.size * cols,
    )[0]


def per_device(
    hidden,
    down_weight,
    down_shrink,
    down_up_factors,
    residual,
    tenant_ids,
    adapter_rank,
    adapter_offset,
    norm_gain,
    qkv_weight,
    qkv_shrink,
    qkv_expand,
):
    my_index = lax.axis_index("tensor")
    z, y = my_index // NY, my_index % NY
    rows, ff = hidden.shape
    share = rows // (NZ * NY)
    width = down_weight.shape[2]
    ranks = down_shrink.shape[2]
    band = NZ * share
    per = ranks // (NZ * NY)
    fence = lax.optimization_barrier
    place = jnp.stack([z, y]).astype(jnp.int32)

    up_own = down_up_factors[0]
    up_near = swap(up_own, 1)
    up_pair = swap(jnp.concatenate([up_own, up_near], axis=0), 2)
    ups = [up_own, up_near, up_pair[: up_own.shape[0]], up_pair[up_own.shape[0] :]]

    far_a, far_b, low_own, *low_parts = far_products(
        place, hidden, down_weight, down_shrink, share
    )
    in_a, in_b = send(far_a, 0, 1), send(far_b, 0, NY - 1)
    low_in = [send(low_parts[d - 1], 0, d) for d in (1, 2, 3)]
    right, left = rest_products(
        place, after(hidden, far_a), down_weight, share, (1, 3)
    )
    my_ids = lax.dynamic_slice_in_dim(tenant_ids.reshape(NZ, NY, share), y, 1, 1).reshape(band)
    my_scale = adapter_scale(my_ids, adapter_rank, adapter_offset, jnp.arange(ranks))
    in_a, in_b, low_in, right, left, my_scale = fence(
        (in_a, in_b, low_in, right, left, my_scale)
    )

    right, left = fold(right, left, in_a, in_b)
    from_left, from_right = send(right, 0, 1), send(left, 0, NY - 1)
    low_y = low_own + sum(part.astype(F32) for part in low_in)
    low_out = low_y.astype(BF)
    low = [low_y] + [send(low_out, e, 0) for e in (2, 1, 3)]
    (own,) = rest_products(place, after(hidden, right), down_weight, share, (0,))
    from_left, from_right, low, my_scale, own, tenant_ids, qkv_expand = fence(
        (from_left, from_right, low, my_scale, own, tenant_ids, qkv_expand)
    )

    pieces = totals(share, place, (own, from_left, from_right), low, my_scale, ups)
    swapped = [send(pieces[e], e, 0) for e in (1, 3, 2)]
    arrived_ids = send(tenant_ids, 0, 0, 1)
    down_own = after(qkv_shrink[0].T, arrived_ids)
    down = [down_own] + [send(down_own, 0, d) for d in (1, 2)]
    swapped, arrived_ids = fence((swapped, arrived_ids))
    block = residual.astype(F32) + pieces[0]
    for part in swapped:
        block = block + part.astype(F32)
    stream = block.astype(BF)

    passed = [send(stream, e, 0, 1) for e in (0, 3, 1, 2)]
    ids = lax.dynamic_slice_in_dim(arrived_ids.reshape(NZ, NY, share), y, 1, 1).reshape(band)
    numbers = z * (NY * per) + jnp.arange(NY * per)
    scale = adapter_scale(ids, adapter_rank, adapter_offset, numbers).T
    expand = qkv_expand[0]
    down.append(send(after(down_own, swapped), 0, 3))
    passed, scale, expand, down = fence((passed, scale, expand, down))
    block, small = normalised(
        share, place, (passed[0], passed[2], passed[3], passed[1]), norm_gain, down, scale
    )

    matrix = qkv_weight[0].T
    from_left, from_right = send(block, 0, 1), send(block, 0, NY - 1)
    small = jnp.concatenate([small] + [send(small, e, 0) for e in (1, 2, 3)], axis=0)
    near = near_products(place, (block,), matrix)
    small = [small] + [send(small, 0, d) for d in (1, 2, 3)]
    from_left, from_right, small, near = fence((from_left, from_right, small, near))
    half = band // 2
    far_a = send(from_left[:half], 0, 1)
    far_b = send(from_right[half:], 0, NY - 1)
    joined = joined_products(share, place, from_right, from_left, matrix, near[0], small, expand)
    far_a, far_b, joined = fence((far_a, far_b, joined))
    out = output_products(share, place, far_a, far_b, matrix, joined)
    return stream, out.T


def solution(mesh):
    in_specs = (
        P("section", "tensor"),
        P("section", "tensor", None),
        P("section", "tensor", None),
        P("section", None, "tensor"),
        P(("section", "tensor"), None),
        P("section"),
        P(),
        P(),
        P("section", None),
        P("section", None, "tensor"),
        P("section", None, "tensor"),
        P("section", None, "tensor"),
    )
    out_specs = (P(("section", "tensor"), None), P("section", "tensor"))
    return jax.shard_map(
        per_device, mesh=mesh, in_specs=in_specs, out_specs=out_specs, check_vma=False
    )
```
